32 devices in a mesh: row: 2 (over core), col: 16 (over z, y, x).
Axes of the slice: x: 2, y: 2, z: 4, core: 2. Of those that a mesh axis runs over, the one named last changes fastest.
Arguments:
- features: bfloat16 [4096, 128], P(('row', 'col')), may hold values from -6 to 6
- weight: bfloat16 [128, 512], replicated, may hold values from -0.5 to 0.5
- bias: float32 [512], replicated, may hold values from -4 to 4
- tile_values: bfloat16 [2, 16, 16, 128, 128], P('row', 'col'), may hold values from 0 to 0.019897461
- tile_index: int32 [2, 16, 16], P('row', 'col'), may hold values from 0 to 31, as said below
- tile_count: int32 [2, 16], P('row', 'col'), may hold values from 2 to 16, as said below
- cotangent: bfloat16 [4096, 512], P(('col', 'row')), may hold values from -20 to 20
Outputs:
- hidden_out: bfloat16 [4096, 512], P(('col', 'row'))
- grad_features: bfloat16 [4096, 128], P(('row', 'col'))
- grad_weight: float32 [128, 512], replicated
- grad_bias: float32 [512], replicated
The draws below stay inside these ranges and needn't reach their ends.
Inputs may be any that keep to these rules, and one draw needn't show every extreme that they name: `tile_index`: within a cell the slots name distinct tiles; slots at or beyond the cell's count hold arbitrary tiles and values. `tile_count`: counts differ from cell to cell; some cell holds exactly 16 live slots.
All inputs are finite; a program needn't handle non-finite values.
Results may differ from the reference program's by a relative error of at most 0.0065.
Values may be sent and summed in bfloat16 or wider, within the bound.
A program may use at most 128 MiB of HBM per device.

```python
import jax
import jax.numpy as jnp
from jax import lax

F = 128
HID = 512
TILE = 128
NODES = 4096
TR = 2
TC = 16
KMAX = 16
N_ROW = 2
N_COL = 16


def draw_tile_index(key, part):
    key = jax.random.fold_in(key, 1)
    keys = jax.random.split(key, N_ROW * N_COL)
    places = jax.vmap(lambda k: jax.random.permutation(k, TR * TC)[:KMAX])(keys)
    return places.reshape(N_ROW, N_COL, KMAX).astype(jnp.int32)


def draw_tile_count(key, part):
    key = jax.random.fold_in(key, 2)
    key_one, key_two, key_three = jax.random.split(key, 3)
    lowest = max(1, KMAX // 8)
    first = jax.random.randint(key_one, (N_ROW * N_COL,), lowest, KMAX + 1)
    second = jax.random.randint(key_two, (N_ROW * N_COL,), lowest, KMAX + 1)
    counts = jnp.minimum(first, second)
    fullest = jax.random.randint(key_three, (), 0, N_ROW * N_COL)
    counts = counts.at[fullest].set(KMAX)
    return counts.reshape(N_ROW, N_COL).astype(jnp.int32)


def draw_cotangent(key, part):
    key = jax.random.fold_in(key, 3)
    place = jnp.arange(NODES, dtype=jnp.float32)[:, None] / NODES
    scale = 3.0 ** place
    values = jnp.clip(jax.random.normal(key, (NODES, HID), jnp.float32), -4.0, 4.0) * scale
    return values.astype(jnp.bfloat16)


def shard_levels(own_key, extent, pieces, smallest, high):
    level, own = 1.0, jax.random.fold_in(own_key, 6)
    for dim, blocks in pieces:
        steps = jnp.exp(jax.random.uniform(jax.random.fold_in(own, dim), (blocks,), jnp.float32, smallest / len(pieces), high / len(pieces)))
        level = level * jnp.repeat(steps, extent[dim] // blocks).reshape([-1 if axis == dim else 1 for axis in range(len(extent))])
    return level


def centred(key, extent, deviation, most, cuts=(), kind=jnp.bfloat16):
    values = deviation * jax.random.normal(key, extent, jnp.float32)
    if cuts:
        values = values * shard_levels(key, extent, cuts, -0.22, 0.18)
    return jnp.clip(values, -most, most).astype(kind)


def setup_inputs(seed: int = 0) -> dict:
    key_list = jax.random.split(jax.random.key(seed), 8)
    return {
        "features": centred(key_list[0], (NODES, F), 1.0, 6.0, ((0, 32),)),
        "weight": centred(key_list[1], (F, HID), F ** -0.5, 0.5),
        "bias": centred(key_list[2], (HID,), 1.0, 4.0, (), jnp.float32),
        "tile_values": jnp.clip(0.019897461 * jax.random.uniform(key_list[3], (N_ROW, N_COL, KMAX, TILE, TILE), jnp.float32) ** shard_levels(key_list[3], (N_ROW, N_COL, KMAX, TILE, TILE), ((0, 2), (1, 16)), -0.2, 0.2), 0.0, 0.019897461).astype(jnp.bfloat16),
        "tile_index": draw_tile_index(jax.random.fold_in(key_list[7], 71), 0),
        "tile_count": draw_tile_count(jax.random.fold_in(key_list[7], 71), 0),
        "cotangent": draw_cotangent(jax.random.fold_in(key_list[7], 71), 0),
    }


def tile_products(tiles, take_idx, put_idx, live, source, count_out, backward):
    picked = jnp.take(source, take_idx, axis=0)
    if backward:
        prod = jnp.einsum("kab,kah->kbh", tiles.astype(jnp.float32), picked.astype(jnp.float32), precision=lax.Precision.HIGHEST)
    else:
        prod = jnp.einsum("kab,kbh->kah", tiles.astype(jnp.float32), picked.astype(jnp.float32), precision=lax.Precision.HIGHEST)
    onehot = ((put_idx[None, :] == jnp.arange(count_out, dtype=jnp.int32)[:, None]) & live[None, :]).astype(jnp.float32)
    return jnp.einsum("tk,kah->tah", onehot, prod, precision=lax.Precision.HIGHEST)


def reference(features, weight, bias, tile_values, tile_index, tile_count, cotangent):
    projected = jnp.dot(features, weight, preferred_element_type=jnp.float32)
    source_rows = TC * TILE
    target_rows = TR * TILE
    slots = jnp.arange(KMAX, dtype=jnp.int32)

    def forward_col(c):
        def add(r, acc):
            idx = tile_index[r, c]
            live = slots < tile_count[r, c]
            block = lax.dynamic_slice_in_dim(projected, (r * source_rows).astype(jnp.int32), source_rows, 0)
            block = block.reshape(TC, TILE, HID)
            return acc + tile_products(tile_values[r, c], idx % TC, idx // TC, live, block, TR, False)
        return lax.fori_loop(0, N_ROW, add, jnp.zeros((TR, TILE, HID), jnp.float32))

    pre = lax.map(forward_col, jnp.arange(N_COL, dtype=jnp.int32)).reshape(NODES, HID) + bias[None, :]
    hidden_out = jax.nn.silu(pre).astype(jnp.bfloat16)
    sig = jax.nn.sigmoid(pre)
    dpre = (cotangent.astype(jnp.float32) * (sig + pre * sig * (1.0 - sig))).astype(jnp.bfloat16)
    grad_bias = jnp.sum(dpre.astype(jnp.float32), axis=0)

    def backward_row(r):
        def add(c, acc):
            idx = tile_index[r, c]
            live = slots < tile_count[r, c]
            block = lax.dynamic_slice_in_dim(dpre, (c * target_rows).astype(jnp.int32), target_rows, 0)
            block = block.reshape(TR, TILE, HID)
            return acc + tile_products(tile_values[r, c], idx // TC, idx % TC, live, block, TC, True)
        return lax.fori_loop(0, N_COL, add, jnp.zeros((TC, TILE, HID), jnp.float32))

    dproj = lax.map(backward_row, jnp.arange(N_ROW, dtype=jnp.int32)).reshape(NODES, HID)
    grad_features = jnp.dot(dproj, weight.astype(jnp.float32).T, precision=lax.Precision.HIGHEST).astype(jnp.bfloat16)
    grad_weight = jnp.dot(features.astype(jnp.float32).T, dproj, precision=lax.Precision.HIGHEST)
    return hidden_out, grad_features, grad_weight, grad_bias
```

```python
import functools

import jax
import jax.numpy as jnp
from jax import lax
from jax.experimental import pallas as pl
from jax.experimental.pallas import tpu as pltpu
from jax.sharding import PartitionSpec as P

MESH = pl.DeviceIdType.MESH
F32 = jnp.float32
BF16 = jnp.bfloat16
GROUP = 16


def nearest_first(count):
    return sorted(range(1, count), key=lambda d: (min(d, count - d), d))


def remote(src, dst, send, recv, device):
    return pltpu.make_async_remote_copy(
        src_ref=src, dst_ref=dst, send_sem=send, recv_sem=recv, device_id=device, device_id_type=MESH
    )


def kernel(
    n_row, n_col, inner,
    features, weight, bias, tiles_in, index, count, cotangent,
    hidden_out, gf_out, gw_out, gb_out,
    x, w, b, tiles, adj, cot, hpart, hid, dpre,
    ssend, srecv, zsend, zrecv, gsend, grecv, gfull, bparts, gf,
    load_sem, store_sem, x_send, x_recv, c_send, c_recv, h_send, h_recv,
    s_send, s_recv, z_send, z_recv, g_send, g_recv, a_send, a_recv, b_send, b_recv,
):
    r = lax.axis_index("row")
    c = lax.axis_index("col")
    outer = n_col // inner
    hi = c // inner
    lo = lax.rem(c, inner)
    rows = features.shape[0]
    own_rows = cot.shape[1]
    width = w.shape[1]
    slots, size = tiles.shape[0], tiles.shape[1]
    tile_cols = n_col * rows // size
    tile_rows = n_row * own_rows // size

    def block(col):
        return pl.ds(pl.multiple_of(col * rows, rows), rows)

    def col_of(turn_hi, turn_lo):
        return lax.rem(hi + turn_hi, outer) * inner + lax.rem(lo + turn_lo, inner)

    load_x = pltpu.make_async_copy(features, x.at[block(c)], load_sem.at[0])
    load_c = pltpu.make_async_copy(cotangent, cot.at[r], load_sem.at[1])
    load_t = pltpu.make_async_copy(tiles_in.at[0, 0], tiles, load_sem.at[2])
    load_w = pltpu.make_async_copy(weight, w, load_sem.at[3])
    load_b = pltpu.make_async_copy(bias, b, load_sem.at[4])
    for load in (load_x, load_c, load_t, load_w, load_b):
        load.start()

    barrier = pltpu.get_barrier_semaphore()
    for d in range(1, n_col):
        pl.semaphore_signal(barrier, inc=1, device_id=(r, lax.rem(c + d, n_col)), device_id_type=MESH)
    for d in range(1, n_row):
        pl.semaphore_signal(barrier, inc=1, device_id=(lax.rem(r + d, n_row), c), device_id_type=MESH)
    pl.semaphore_wait(barrier, n_col + n_row - 2)

    pending = []

    def send(copy):
        copy.start()
        pending.append(copy)

    def send_x(number, source, to):
        send(remote(x.at[block(source)], x.at[block(source)], x_send.at[number], x_recv.at[source], (r, to)))

    def wait_x(source):
        remote(x.at[block(source)], x.at[block(source)], x_send.at[0], x_recv.at[source], (r, c)).wait_recv()

    number = 0
    load_x.wait()
    for d in nearest_first(outer):
        send_x(number, c, col_of(d, 0))
        number += 1
    for q in range(1, inner):
        send_x(number, c, col_of(0, q))
        number += 1
    load_c.wait()
    for d in range(1, n_row):
        send(remote(cot.at[r], cot.at[r], c_send.at[d], c_recv.at[r], (lax.rem(r + d, n_row), c)))

    load_t.wait()
    live = count[0, 0]

    def place(t, carry):
        def find(s, slot):
            return jnp.where((index[0, 0, s] == t) & (s < live), s, slot)

        slot = lax.fori_loop(0, slots, find, jnp.int32(-1), unroll=min(slots, 16))
        tile = tiles[jnp.maximum(slot, 0)]
        row = pl.ds(pl.multiple_of(t // tile_cols * size, size), size)
        column = pl.ds(pl.multiple_of(lax.rem(t, tile_cols) * size, size), size)
        adj[row, column] = jnp.where(slot >= 0, tile, jnp.zeros_like(tile))
        return carry

    lax.fori_loop(0, tile_rows * tile_cols, place, 0)

    for d in nearest_first(outer):
        source = col_of(d, 0)
        wait_x(source)
        for q in range(1, inner):
            send_x(number, source, col_of(0, q))
            number += 1
    for d in [0] + nearest_first(outer):
        for q in range(1, inner):
            wait_x(col_of(d, q))

    total_rows = n_row * own_rows
    step = min(256, total_rows)
    for at in range(0, total_rows, step):
        hpart[r, at : at + step, :] = jnp.dot(adj[at : at + step, :], x[...], preferred_element_type=F32)
    for d in range(1, n_row):
        send(remote(hpart.at[r], hpart.at[r], h_send.at[d], h_recv.at[r], (lax.rem(r + d, n_row), c)))
    load_w.wait()
    load_b.wait()
    for d in range(1, n_row):
        other = lax.rem(r + d, n_row)
        remote(cot.at[other], cot.at[other], c_send.at[0], c_recv.at[other], (r, c)).wait_recv()
    for d in range(1, n_row):
        other = lax.rem(r + d, n_row)
        remote(hpart.at[other], hpart.at[other], h_send.at[0], h_recv.at[other], (r, c)).wait_recv()
    h = hpart[0]
    for k in range(1, n_row):
        h = h + hpart[k]
    hb = h.astype(BF16)
    ht = h.T.astype(BF16)

    bias_sum = jnp.zeros((1, width), F32)
    for k in range(n_row):
        part = hb[k * own_rows : (k + 1) * own_rows]
        pre = jnp.dot(part, w[...], preferred_element_type=F32) + b[...]
        sig = jax.nn.sigmoid(pre)
        hid[k] = (pre * sig).astype(BF16)
        grad = (cot[k].astype(F32) * (sig + pre * sig * (1.0 - sig))).astype(BF16)
        dpre[k * own_rows : (k + 1) * own_rows, :] = grad
        bias_sum = bias_sum + jnp.sum(grad.astype(F32), axis=0, keepdims=True)
    store_h = pltpu.make_async_copy(hid.at[r], hidden_out, store_sem.at[0])
    store_h.start()

    gt = lax.dot_general(w[...], dpre[...], (((1,), (1,)), ((), ())), preferred_element_type=F32).astype(BF16)
    lanes = inner * rows
    for d in nearest_first(outer) + [0]:
        to = lax.rem(hi + d, outer)
        columns = pl.ds(pl.multiple_of(to * lanes, lanes), lanes)
        part = jnp.dot(gt, adj[:, columns], preferred_element_type=F32).astype(BF16)
        for q in range(inner):
            ssend[d, q] = part[:, q * rows : (q + 1) * rows]
        for q in range(1, inner):
            at = lax.rem(lo + q, inner)
            send(remote(ssend.at[d, at], srecv.at[d, lo], s_send.at[d, q], s_recv.at[d, lo], (r, hi * inner + at)))

    gw = jnp.dot(ht, dpre[...], preferred_element_type=F32).astype(BF16)
    chunk = gsend.shape[2]
    parts = width // chunk
    for k in range(n_col):
        g, l = k // parts, k % parts
        gsend[k] = gw[g * GROUP : (g + 1) * GROUP, l * chunk : (l + 1) * chunk]
    bparts[c] = bias_sum
    grecv[c] = gsend[c]
    for d in range(1, n_col):
        to = lax.rem(c + d, n_col)
        send(remote(gsend.at[to], grecv.at[c], g_send.at[d], g_recv.at[c], (r, to)))
    for d in range(1, n_col):
        to = lax.rem(c + d, n_col)
        send(remote(bparts.at[c], bparts.at[c], b_send.at[d], b_recv.at[c], (r, to)))

    own_sum = None
    for d in nearest_first(outer) + [0]:
        for q in range(1, inner):
            at = lax.rem(lo + q, inner)
            remote(ssend.at[d, at], srecv.at[d, at], s_send.at[0, 0], s_recv.at[d, at], (r, c)).wait_recv()
        part = ssend[d, lo].astype(F32)
        for q in range(1, inner):
            part = part + srecv[d, lax.rem(lo + q, inner)].astype(F32)
        if d:
            to = lax.rem(hi + d, outer)
            zsend[d] = part.astype(BF16)
            send(remote(zsend.at[d], zrecv.at[hi], z_send.at[d], z_recv.at[hi], (r, to * inner + lo)))
        else:
            own_sum = part

    for d in range(1, n_col):
        source = lax.rem(c + d, n_col)
        remote(gsend.at[0], grecv.at[source], g_send.at[0], g_recv.at[source], (r, c)).wait_recv()
    total = grecv[0].astype(F32)
    for k in range(1, n_col):
        total = total + grecv[k].astype(F32)
    gfull[c] = total.astype(BF16)
    for d in range(1, n_col):
        to = lax.rem(c + d, n_col)
        send(remote(gfull.at[c], gfull.at[c], a_send.at[d], a_recv.at[c], (r, to)))

    for d in nearest_first(outer):
        source = lax.rem(hi + d, outer)
        remote(zsend.at[0], zrecv.at[source], z_send.at[0], z_recv.at[source], (r, c)).wait_recv()
        own_sum = own_sum + zrecv[source].astype(F32)
    gf[...] = own_sum.T.astype(BF16)
    store_f = pltpu.make_async_copy(gf, gf_out, store_sem.at[1])
    store_f.start()

    for d in range(1, n_col):
        source = lax.rem(c + d, n_col)
        remote(bparts.at[source], bparts.at[source], b_send.at[0], b_recv.at[source], (r, c)).wait_recv()
    bias_total = bparts[0]
    for k in range(1, n_col):
        bias_total = bias_total + bparts[k]
    gb_out[...] = bias_total
    for d in range(1, n_col):
        source = lax.rem(c + d, n_col)
        remote(gfull.at[source], gfull.at[source], a_send.at[0], a_recv.at[source], (r, c)).wait_recv()
    for k in range(n_col):
        g, l = k // parts, k % parts
        gw_out[g * GROUP : (g + 1) * GROUP, l * chunk : (l + 1) * chunk] = gfull[k].astype(F32)
    for copy in pending:
        copy.wait_send()
    store_h.wait()
    store_f.wait()


def local(n_row, n_col, features, weight, bias, tile_values, tile_index, tile_count, cotangent):
    rows, feat = features.shape
    own_rows, width = cotangent.shape
    slots, size = tile_values.shape[2], tile_values.shape[3]
    inner = 4
    outer = n_col // inner
    target = n_row * own_rows
    source = n_col * rows
    chunk = feat * width // (GROUP * n_col)
    dma = pltpu.SemaphoreType.DMA
    any_spec = pl.BlockSpec(memory_space=pl.ANY)
    smem = pl.BlockSpec(memory_space=pltpu.SMEM)
    vmem = pl.BlockSpec(memory_space=pltpu.VMEM)
    hidden, gf, gw, gb = pl.pallas_call(
        functools.partial(kernel, n_row, n_col, inner),
        out_shape=(
            jax.ShapeDtypeStruct((own_rows, width), BF16),
            jax.ShapeDtypeStruct((rows, feat), BF16),
            jax.ShapeDtypeStruct((feat, width), F32),
            jax.ShapeDtypeStruct((1, width), F32),
        ),
        in_specs=[any_spec, any_spec, any_spec, any_spec, smem, smem, any_spec],
        out_specs=(any_spec, any_spec, vmem, vmem),
        scratch_shapes=[
            pltpu.VMEM((source, feat), BF16),
            pltpu.VMEM((feat, width), BF16),
            pltpu.VMEM((1, width), F32),
            pltpu.VMEM((slots, size, size), BF16),
            pltpu.VMEM((target, source), BF16),
            pltpu.VMEM((n_row, own_rows, width), BF16),
            pltpu.VMEM((n_row, target, feat), F32),
            pltpu.VMEM((n_row, own_rows, width), BF16),
            pltpu.VMEM((target, width), BF16),
            pltpu.VMEM((outer, inner, feat, rows), BF16),
            pltpu.VMEM((outer, inner, feat, rows), BF16),
            pltpu.VMEM((outer, feat, rows), BF16),
            pltpu.VMEM((outer, feat, rows), BF16),
            pltpu.VMEM((n_col, GROUP, chunk), BF16),
            pltpu.VMEM((n_col, GROUP, chunk), BF16),
            pltpu.VMEM((n_col, GROUP, chunk), BF16),
            pltpu.VMEM((n_col, 1, width), F32),
            pltpu.VMEM((rows, feat), BF16),
            dma((5,)), dma((2,)),
            dma((n_col,)), dma((n_col,)),
            dma((n_row,)), dma((n_row,)),
            dma((n_row,)), dma((n_row,)),
            dma((outer, inner)), dma((outer, inner)),
            dma((outer,)), dma((outer,)),
            dma((n_col,)), dma((n_col,)),
            dma((n_col,)), dma((n_col,)),
            dma((n_col,)), dma((n_col,)),
        ],
        compiler_params=pltpu.CompilerParams(
            collective_id=0, has_side_effects=True, vmem_limit_bytes=48 * 1024 * 1024
        ),
        cost_estimate=pl.CostEstimate(
            flops=4 * target * source * feat + 6 * target * width * feat,
            bytes_accessed=2 * (slots * size * size + 3 * own_rows * width),
            transcendentals=target * width,
        ),
    )(features, weight, bias.reshape(1, width), tile_values, tile_index, tile_count, cotangent)
    return hidden, gf, gw, gb.reshape(width)


def solution(mesh):
    in_specs = (
        P(("row", "col"), None),
        P(),
        P(),
        P("row", "col", None, None, None),
        P("row", "col", None),
        P("row", "col"),
        P(("col", "row"), None),
    )
    out_specs = (P(("col", "row"), None), P(("row", "col"), None), P(), P())
    body = functools.partial(local, mesh.shape["row"], mesh.shape["col"])
    return jax.shard_map(body, mesh=mesh, in_specs=in_specs, out_specs=out_specs, check_vma=False)
```

```python
import functools

import jax
import jax.numpy as jnp
from jax import lax
from jax.experimental import pallas as pl
from jax.experimental.pallas import tpu as pltpu
from jax.sharding import PartitionSpec as P

MESH = pl.DeviceIdType.MESH
F32 = jnp.float32
BF16 = jnp.bfloat16
GROUP = 16


def nearest_first(count):
    return sorted(range(1, count), key=lambda d: (min(d, count - d), d))


def remote(src, dst, send, recv, device):
    return pltpu.make_async_remote_copy(
        src_ref=src, dst_ref=dst, send_sem=send, recv_sem=recv, device_id=device, device_id_type=MESH
    )


def kernel(
    n_row, n_col, inner, split,
    features, weight, bias, tiles_in, index_in, count, cotangent,
    hidden_out, gf_out, gw_out, gb_out,
    x, w, b, tiles, adj, cot, hpart, hts, hid, dpre,
    ssend, srecv, zsend, zrecv, gsend, grecv, gfull, bparts, gf, index,
    load_sem, store_sem, x_send, x_recv, c_send, c_recv, h_send, h_recv,
    s_send, s_recv, z_send, z_recv, g_send, g_recv, a_send, a_recv, b_send, b_recv, p_send, p_recv,
):
    r = lax.axis_index("row")
    c = lax.axis_index("col")
    outer = n_col // inner
    hi = c // inner
    lo = lax.rem(c, inner)
    swap = lax.rem(r, 2) if outer == inner else 0
    a = hi + swap * (lo - hi)
    b_at = lo + swap * (hi - lo)

    def col_at(first, second):
        return (first + swap * (second - first)) * inner + second + swap * (first - second)

    def place_of(col):
        high, low = col // inner, lax.rem(col, inner)
        return (high + swap * (low - high)) * inner + low + swap * (high - low)

    me = a * inner + b_at
    rows = features.shape[0]
    own_rows = cot.shape[1]
    width = w.shape[1]
    slots, size = tiles.shape[0], tiles.shape[1]
    tile_cols = n_col * rows // size
    tile_rows = n_row * own_rows // size

    def block(spot):
        return pl.ds(pl.multiple_of(spot * rows, rows), rows)

    def turned(turn_a, turn_b):
        return lax.rem(a + turn_a, outer), lax.rem(b_at + turn_b, inner)

    def spot_of(turn_a, turn_b):
        first, second = turned(turn_a, turn_b)
        return first * inner + second

    def col_of(turn_a, turn_b):
        return col_at(*turned(turn_a, turn_b))

    load_x = pltpu.make_async_copy(features, x.at[block(me)], load_sem.at[0])
    load_c = pltpu.make_async_copy(cotangent, cot.at[r], load_sem.at[1])
    load_t = pltpu.make_async_copy(tiles_in.at[0, 0], tiles, load_sem.at[2])
    load_w = pltpu.make_async_copy(weight, w, load_sem.at[3])
    load_b = pltpu.make_async_copy(bias, b, load_sem.at[4])
    load_i = pltpu.make_async_copy(index_in, index, load_sem.at[5])
    for load in (load_x, load_c, load_t, load_w, load_b, load_i):
        load.start()

    barrier = pltpu.get_barrier_semaphore()
    for d in range(1, n_col):
        pl.semaphore_signal(barrier, inc=1, device_id=(r, lax.rem(c + d, n_col)), device_id_type=MESH)
    for d in range(1, n_row):
        pl.semaphore_signal(barrier, inc=1, device_id=(lax.rem(r + d, n_row), c), device_id_type=MESH)
    pl.semaphore_wait(barrier, n_col + n_row - 2)

    pending = []

    def send(copy):
        copy.start()
        pending.append(copy)

    def send_x(number, source, to):
        send(remote(x.at[block(source)], x.at[block(source)], x_send.at[number], x_recv.at[source], (r, to)))

    def wait_x(source):
        remote(x.at[block(source)], x.at[block(source)], x_send.at[0], x_recv.at[source], (r, c)).wait_recv()

    number = 0
    load_x.wait()
    for d in nearest_first(outer):
        send_x(number, me, col_of(d, 0))
        number += 1
    for q in range(1, inner):
        send_x(number, me, col_of(0, q))
        number += 1
    load_c.wait()
    for d in range(1, n_row):
        send(remote(cot.at[r], cot.at[r], c_send.at[d], c_recv.at[r], (lax.rem(r + d, n_row), c)))

    load_t.wait()
    load_i.wait()
    live = count[0, 0]

    def place(t, carry):
        def find(s, slot):
            return jnp.where((index[0, 0, s] == t) & (s < live), s, slot)

        slot = lax.fori_loop(0, slots, find, jnp.int32(-1), unroll=min(slots, 16))
        tile = tiles[jnp.maximum(slot, 0)]
        row = pl.ds(pl.multiple_of(t // tile_cols * size, size), size)
        column = pl.ds(pl.multiple_of(place_of(lax.rem(t, tile_cols)) * size, size), size)
        adj[row, column] = jnp.where(slot >= 0, tile, jnp.zeros_like(tile))
        return carry

    lax.fori_loop(0, tile_rows * tile_cols, place, 0)

    for d in nearest_first(outer):
        source = spot_of(d, 0)
        wait_x(source)
        for q in range(1, inner):
            send_x(number, source, col_of(0, q))
            number += 1
    for d in [0] + nearest_first(outer):
        for q in range(1, inner):
            wait_x(spot_of(d, q))

    total_rows = n_row * own_rows
    step = min(256, total_rows)
    for at in range(0, total_rows, step):
        hpart[r, at : at + step, :] = jnp.dot(adj[at : at + step, :], x[...], preferred_element_type=F32)
    for d in range(1, n_row):
        send(remote(hpart.at[r], hpart.at[r], h_send.at[d], h_recv.at[r], (lax.rem(r + d, n_row), c)))
    load_w.wait()
    load_b.wait()
    for d in range(1, n_row):
        other = lax.rem(r + d, n_row)
        remote(cot.at[other], cot.at[other], c_send.at[0], c_recv.at[other], (r, c)).wait_recv()
    for d in range(1, n_row):
        other = lax.rem(r + d, n_row)
        remote(hpart.at[other], hpart.at[other], h_send.at[0], h_recv.at[other], (r, c)).wait_recv()
    h = hpart[0]
    for k in range(1, n_row):
        h = h + hpart[k]
    hb = h.astype(BF16)
    hts[...] = h.T.astype(BF16)

    bias_sum = jnp.zeros((1, width), F32)
    for k in range(n_row):
        part = hb[k * own_rows : (k + 1) * own_rows]
        pre = jnp.dot(part, w[...], preferred_element_type=F32) + b[...]
        sig = jax.nn.sigmoid(pre)
        hid[k] = (pre * sig).astype(BF16)
        grad = (cot[k].astype(F32) * (sig + pre * sig * (1.0 - sig))).astype(BF16)
        dpre[k * own_rows : (k + 1) * own_rows, :] = grad
        bias_sum = bias_sum + jnp.sum(grad.astype(F32), axis=0, keepdims=True)
    store_h = pltpu.make_async_copy(hid.at[r], hidden_out, store_sem.at[0])
    store_h.start()

    half = lax.rem(r, split)
    deep = hts.shape[0] // split
    gw = jnp.dot(hts[pl.ds(pl.multiple_of(half * deep, deep), deep), :], dpre[...], preferred_element_type=F32).astype(BF16)
    chunk = gsend.shape[2]
    parts = width // chunk
    for k in range(n_col):
        g, l = k // parts, k % parts
        gsend[k] = gw[g * GROUP : (g + 1) * GROUP, l * chunk : (l + 1) * chunk]
    bparts[c] = bias_sum
    grecv[c] = gsend[c]
    for d in range(1, n_col):
        to = lax.rem(c + d, n_col)
        send(remote(gsend.at[to], grecv.at[c], g_send.at[d], g_recv.at[c], (r, to)))

    gt = lax.dot_general(w[...], dpre[...], (((1,), (1,)), ((), ())), preferred_element_type=F32).astype(BF16)
    lanes = inner * rows
    for d in nearest_first(outer) + [0]:
        to = lax.rem(a + d, outer)
        columns = pl.ds(pl.multiple_of(to * lanes, lanes), lanes)
        part = jnp.dot(gt, adj[:, columns], preferred_element_type=F32).astype(BF16)
        for q in range(inner):
            ssend[d, q] = part[:, q * rows : (q + 1) * rows]
        for q in range(1, inner):
            at = lax.rem(b_at + q, inner)
            send(remote(ssend.at[d, at], srecv.at[d, b_at], s_send.at[d, q], s_recv.at[d, b_at], (r, col_at(a, at))))

    for d in range(1, n_col):
        to = lax.rem(c + d, n_col)
        send(remote(bparts.at[c], bparts.at[c], b_send.at[d], b_recv.at[c], (r, to)))

    for d in range(1, n_col):
        source = lax.rem(c + d, n_col)
        remote(gsend.at[0], grecv.at[source], g_send.at[0], g_recv.at[source], (r, c)).wait_recv()
    total = grecv[0].astype(F32)
    for k in range(1, n_col):
        total = total + grecv[k].astype(F32)
    gfull[half, c] = total.astype(BF16)
    for d in range(1, n_col):
        to = lax.rem(c + d, n_col)
        send(remote(gfull.at[half, c], gfull.at[half, c], a_send.at[d], a_recv.at[c], (r, to)))

    own_sum = None
    for d in nearest_first(outer) + [0]:
        for q in range(1, inner):
            at = lax.rem(b_at + q, inner)
            remote(ssend.at[d, at], srecv.at[d, at], s_send.at[0, 0], s_recv.at[d, at], (r, c)).wait_recv()
        part = ssend[d, b_at].astype(F32)
        for q in range(1, inner):
            part = part + srecv[d, lax.rem(b_at + q, inner)].astype(F32)
        if d:
            to = lax.rem(a + d, outer)
            zsend[d] = part.astype(BF16)
            send(remote(zsend.at[d], zrecv.at[a], z_send.at[d], z_recv.at[a], (r, col_at(to, b_at))))
        else:
            own_sum = part

    for d in range(1, n_col):
        source = lax.rem(c + d, n_col)
        remote(gfull.at[half, source], gfull.at[half, source], a_send.at[0], a_recv.at[source], (r, c)).wait_recv()
    if split == 2:
        partner = r + 1 - 2 * half
        send(remote(gfull.at[half], gfull.at[half], p_send.at[0], p_recv.at[0], (partner, c)))
    for d in nearest_first(outer):
        source = lax.rem(a + d, outer)
        remote(zsend.at[0], zrecv.at[source], z_send.at[0], z_recv.at[source], (r, c)).wait_recv()
        own_sum = own_sum + zrecv[source].astype(F32)
    gf[...] = own_sum.T.astype(BF16)
    store_f = pltpu.make_async_copy(gf, gf_out, store_sem.at[1])
    store_f.start()

    for d in range(1, n_col):
        source = lax.rem(c + d, n_col)
        remote(bparts.at[source], bparts.at[source], b_send.at[0], b_recv.at[source], (r, c)).wait_recv()
    bias_total = bparts[0]
    for k in range(1, n_col):
        bias_total = bias_total + bparts[k]
    gb_out[...] = bias_total
    if split == 2:
        remote(gfull.at[1 - half], gfull.at[1 - half], p_send.at[0], p_recv.at[0], (r, c)).wait_recv()
    for n in range(split):
        for k in range(n_col):
            top, l = n * deep + k // parts * GROUP, k % parts
            gw_out[top : top + GROUP, l * chunk : (l + 1) * chunk] = gfull[n, k].astype(F32)
    for copy in pending:
        copy.wait_send()
    store_h.wait()
    store_f.wait()


def hand_over(*refs):
    sources, results, sems = refs[:4], refs[4:8], refs[8]
    copies = [pltpu.make_async_copy(sources[k], results[k], sems.at[k]) for k in range(4)]
    for copy in copies:
        copy.start()
    for copy in copies:
        copy.wait()


def local(n_row, n_col, features, weight, bias, tile_values, tile_index, tile_count, cotangent):
    rows, feat = features.shape
    own_rows, width = cotangent.shape
    slots, size = tile_values.shape[2], tile_values.shape[3]
    inner = 4
    outer = n_col // inner
    target = n_row * own_rows
    source = n_col * rows
    chunk = feat * width // (GROUP * n_col)
    split = 2 if n_row % 2 == 0 and chunk % 256 == 0 else 1
    chunk = chunk // split
    dma = pltpu.SemaphoreType.DMA
    any_spec = pl.BlockSpec(memory_space=pl.ANY)
    hbm = pl.BlockSpec(memory_space=pltpu.HBM)
    vmem = pl.BlockSpec(memory_space=pltpu.VMEM)
    hidden, gf, gw, gb = pl.pallas_call(
        functools.partial(kernel, n_row, n_col, inner, split),
        out_shape=(
            jax.ShapeDtypeStruct((own_rows, width), BF16),
            jax.ShapeDtypeStruct((rows, feat), BF16),
            jax.ShapeDtypeStruct((feat, width), F32),
            jax.ShapeDtypeStruct((1, width), F32),
        ),
        in_specs=[hbm] * 5 + [pl.BlockSpec(memory_space=pltpu.SMEM), hbm],
        out_specs=(any_spec, any_spec, vmem, vmem),
        scratch_shapes=[
            pltpu.VMEM((source, feat), BF16),
            pltpu.VMEM((feat, width), BF16),
            pltpu.VMEM((1, width), F32),
            pltpu.VMEM((slots, size, size), BF16),
            pltpu.VMEM((target, source), BF16),
            pltpu.VMEM((n_row, own_rows, width), BF16),
            pltpu.VMEM((n_row, target, feat), F32),
            pltpu.VMEM((feat, target), BF16),
            pltpu.VMEM((n_row, own_rows, width), BF16),
            pltpu.VMEM((target, width), BF16),
            pltpu.VMEM((outer, inner, feat, rows), BF16),
            pltpu.VMEM((outer, inner, feat, rows), BF16),
            pltpu.VMEM((outer, feat, rows), BF16),
            pltpu.VMEM((outer, feat, rows), BF16),
            pltpu.VMEM((n_col, GROUP, chunk), BF16),
            pltpu.VMEM((n_col, GROUP, chunk), BF16),
            pltpu.VMEM((split, n_col, GROUP, chunk), BF16),
            pltpu.VMEM((n_col, 1, width), F32),
            pltpu.VMEM((rows, feat), BF16),
            pltpu.SMEM(tile_index.shape, jnp.int32),
            dma((6,)), dma((2,)),
            dma((n_col,)), dma((n_col,)),
            dma((n_row,)), dma((n_row,)),
            dma((n_row,)), dma((n_row,)),
            dma((outer, inner)), dma((outer, inner)),
            dma((outer,)), dma((outer,)),
            dma((n_col,)), dma((n_col,)),
            dma((n_col,)), dma((n_col,)),
            dma((n_col,)), dma((n_col,)),
            dma((1,)), dma((1,)),
        ],
        compiler_params=pltpu.CompilerParams(
            collective_id=0, has_side_effects=True, vmem_limit_bytes=60 * 1024 * 1024
        ),
        cost_estimate=pl.CostEstimate(
            flops=4 * target * source * feat + 6 * target * width * feat,
            bytes_accessed=2 * (slots * size * size + 3 * own_rows * width),
            transcendentals=target * width,
        ),
    )(features, weight, bias.reshape(1, width), tile_values, tile_index, tile_count, cotangent)
    results = (hidden, gf, gw, gb)
    hidden, gf, gw, gb = pl.pallas_call(
        hand_over,
        out_shape=tuple(jax.ShapeDtypeStruct(value.shape, value.dtype) for value in results),
        in_specs=[any_spec] * 4,
        out_specs=(any_spec,) * 4,
        scratch_shapes=[dma((4,))],
        compiler_params=pltpu.CompilerParams(vmem_limit_bytes=60 * 1024 * 1024),
    )(*results)
    return hidden, gf, gw, gb.reshape(width)


def solution(mesh):
    in_specs = (
        P(("row", "col"), None),
        P(),
        P(),
        P("row", "col", None, None, None),
        P("row", "col", None),
        P("row", "col"),
        P(("col", "row"), None),
    )
    out_specs = (P(("col", "row"), None), P(("row", "col"), None), P(), P())
    body = functools.partial(local, mesh.shape["row"], mesh.shape["col"])
    return jax.shard_map(body, mesh=mesh, in_specs=in_specs, out_specs=out_specs, check_vma=False)
```

```python
import functools

import jax
import jax.numpy as jnp
from jax import lax
from jax.experimental import pallas as pl
from jax.experimental.pallas import tpu as pltpu
from jax.sharding import PartitionSpec as P

MESH = pl.DeviceIdType.MESH
F32 = jnp.float32
BF16 = jnp.bfloat16
GROUP = 16


def nearest_first(count):
    return sorted(range(1, count), key=lambda d: (min(d, count - d), d))


def remote(src, dst, send, recv, device):
    return pltpu.make_async_remote_copy(
        src_ref=src, dst_ref=dst, send_sem=send, recv_sem=recv, device_id=device, device_id_type=MESH
    )


def kernel(
    n_row, n_col, inner, split,
    features, weight, bias, tiles_in, index_in, count, cotangent,
    hidden_out, gf_out, gw_out, gb_out,
    x, w, b, tiles, adj, cot, hpart, hts, hid, dpre,
    ssend, srecv, zsend, zrecv, gsend, grecv, gfull, bparts, bouter, gb, gf, index,
    load_sem, store_sem, x_send, x_recv, c_send, c_recv, h_send, h_recv,
    s_send, s_recv, z_send, z_recv, g_send, g_recv, a_send, a_recv, b_send, b_recv, p_send, p_recv, d_send, d_recv,
):
    r = lax.axis_index("row")
    c = lax.axis_index("col")
    outer = n_col // inner
    hi = c // inner
    lo = lax.rem(c, inner)
    swap = lax.rem(r, 2) if outer == inner else 0
    a = hi + swap * (lo - hi)
    b_at = lo + swap * (hi - lo)

    def col_at(first, second):
        return (first + swap * (second - first)) * inner + second + swap * (first - second)

    def place_of(col):
        high, low = col // inner, lax.rem(col, inner)
        return (high + swap * (low - high)) * inner + low + swap * (high - low)

    me = a * inner + b_at
    rows = features.shape[0]
    own_rows = cot.shape[1]
    width = w.shape[1]
    slots, size = tiles.shape[0], tiles.shape[1]
    tile_cols = n_col * rows // size
    tile_rows = n_row * own_rows // size

    def block(spot):
        return pl.ds(pl.multiple_of(spot * rows, rows), rows)

    def turned(turn_a, turn_b):
        return lax.rem(a + turn_a, outer), lax.rem(b_at + turn_b, inner)

    def spot_of(turn_a, turn_b):
        first, second = turned(turn_a, turn_b)
        return first * inner + second

    def col_of(turn_a, turn_b):
        return col_at(*turned(turn_a, turn_b))

    load_x = pltpu.make_async_copy(features, x.at[block(me)], load_sem.at[0])
    load_c = pltpu.make_async_copy(cotangent, cot.at[r], load_sem.at[1])
    load_t = pltpu.make_async_copy(tiles_in.at[0, 0], tiles, load_sem.at[2])
    load_w = pltpu.make_async_copy(weight, w, load_sem.at[3])
    load_b = pltpu.make_async_copy(bias, b, load_sem.at[4])
    load_i = pltpu.make_async_copy(index_in, index, load_sem.at[5])
    for load in (load_x, load_c, load_t, load_w, load_b, load_i):
        load.start()

    barrier = pltpu.get_barrier_semaphore()
    for d in range(1, n_col):
        pl.semaphore_signal(barrier, inc=1, device_id=(r, lax.rem(c + d, n_col)), device_id_type=MESH)
    for d in range(1, n_row):
        pl.semaphore_signal(barrier, inc=1, device_id=(lax.rem(r + d, n_row), c), device_id_type=MESH)
    pl.semaphore_wait(barrier, n_col + n_row - 2)

    pending = []

    def send(copy):
        copy.start()
        pending.append(copy)

    def sent():
        for copy in pending:
            copy.wait_send()
        pending.clear()

    def send_x(number, source, to):
        send(remote(x.at[block(source)], x.at[block(source)], x_send.at[number], x_recv.at[source], (r, to)))

    def wait_x(source):
        remote(x.at[block(source)], x.at[block(source)], x_send.at[0], x_recv.at[source], (r, c)).wait_recv()

    number = 0
    load_x.wait()
    for d in nearest_first(outer):
        send_x(number, me, col_of(d, 0))
        number += 1
    for q in range(1, inner):
        send_x(number, me, col_of(0, q))
        number += 1
    load_c.wait()
    for d in range(1, n_row):
        send(remote(cot.at[r], cot.at[r], c_send.at[d], c_recv.at[r], (lax.rem(r + d, n_row), c)))

    load_t.wait()
    load_i.wait()
    live = count[0, 0]

    def place(t, carry):
        def find(s, slot):
            return jnp.where((index[0, 0, s] == t) & (s < live), s, slot)

        slot = lax.fori_loop(0, slots, find, jnp.int32(-1), unroll=min(slots, 16))
        tile = tiles[jnp.maximum(slot, 0)]
        row = pl.ds(pl.multiple_of(t // tile_cols * size, size), size)
        column = pl.ds(pl.multiple_of(place_of(lax.rem(t, tile_cols)) * size, size), size)
        adj[row, column] = jnp.where(slot >= 0, tile, jnp.zeros_like(tile))
        return carry

    lax.fori_loop(0, tile_rows * tile_cols, place, 0)

    for d in nearest_first(outer):
        source = spot_of(d, 0)
        wait_x(source)
        for q in range(1, inner):
            send_x(number, source, col_of(0, q))
            number += 1
    span = inner * rows
    partial = None
    for d in [0] + nearest_first(outer):
        for q in range(1, inner):
            wait_x(spot_of(d, q))
        group = pl.ds(pl.multiple_of(lax.rem(a + d, outer) * span, span), span)
        part = jnp.dot(adj[:, group], x[group, :], preferred_element_type=F32)
        partial = part if partial is None else partial + part
    hpart[r] = partial
    for d in range(1, n_row):
        send(remote(hpart.at[r], hpart.at[r], h_send.at[d], h_recv.at[r], (lax.rem(r + d, n_row), c)))
    load_w.wait()
    load_b.wait()
    for d in range(1, n_row):
        other = lax.rem(r + d, n_row)
        remote(cot.at[other], cot.at[other], c_send.at[0], c_recv.at[other], (r, c)).wait_recv()
    for d in range(1, n_row):
        other = lax.rem(r + d, n_row)
        remote(hpart.at[other], hpart.at[other], h_send.at[0], h_recv.at[other], (r, c)).wait_recv()
    h = hpart[0]
    for k in range(1, n_row):
        h = h + hpart[k]
    hb = h.astype(BF16)
    hts[...] = h.T.astype(BF16)

    bias_sum = jnp.zeros((1, width), F32)
    for k in range(n_row):
        part = hb[k * own_rows : (k + 1) * own_rows]
        pre = jnp.dot(part, w[...], preferred_element_type=F32) + b[...]
        sig = 0.5 * jnp.tanh(0.5 * pre) + 0.5
        hid[k] = (pre * sig).astype(BF16)
        grad = (cot[k].astype(F32) * (sig + pre * sig * (1.0 - sig))).astype(BF16)
        dpre[k * own_rows : (k + 1) * own_rows, :] = grad
        bias_sum = bias_sum + jnp.sum(grad.astype(F32), axis=0, keepdims=True)
    store_h = pltpu.make_async_copy(hid.at[r], hidden_out, store_sem.at[0])
    store_h.start()

    half = lax.rem(r, split)
    deep = hts.shape[0] // split
    gw = jnp.dot(hts[pl.ds(pl.multiple_of(half * deep, deep), deep), :], dpre[...], preferred_element_type=F32).astype(BF16)
    chunk = gsend.shape[2]
    parts = width // chunk
    for k in range(n_col):
        g, l = k // parts, k % parts
        gsend[k] = gw[g * GROUP : (g + 1) * GROUP, l * chunk : (l + 1) * chunk]
    grecv[c] = gsend[c]
    for d in range(1, n_col):
        to = lax.rem(c + d, n_col)
        send(remote(gsend.at[to], grecv.at[c], g_send.at[d], g_recv.at[c], (r, to)))

    gt = lax.dot_general(w[...], dpre[...], (((1,), (1,)), ((), ())), preferred_element_type=F32).astype(BF16)
    order = nearest_first(outer) + [0]
    portion = max(1, outer // 2)
    for n, d in enumerate(order):
        columns = pl.ds(pl.multiple_of(lax.rem(a + d, outer) * span, span), span)
        part = jnp.dot(gt, adj[:, columns], preferred_element_type=F32).astype(BF16)
        for q in range(inner):
            ssend[q, n] = part[:, q * rows : (q + 1) * rows]
        if (n + 1) % portion == 0:
            run, m = pl.ds(n + 1 - portion, portion), n // portion
            for q in range(1, inner):
                at = lax.rem(b_at + q, inner)
                send(remote(ssend.at[at, run], srecv.at[b_at, run], s_send.at[m, q], s_recv.at[m, b_at], (r, col_at(a, at))))
    bparts[lo] = bias_sum
    for q in range(1, inner):
        at = lax.rem(lo + q, inner)
        send(remote(bparts.at[lo], bparts.at[lo], b_send.at[q], b_recv.at[lo], (r, hi * inner + at)))

    for d in range(1, n_col):
        source = lax.rem(c + d, n_col)
        remote(gsend.at[0], grecv.at[source], g_send.at[0], g_recv.at[source], (r, c)).wait_recv()
    total = grecv[0].astype(F32)
    for k in range(1, n_col):
        total = total + grecv[k].astype(F32)
    gfull[half, c] = total.astype(BF16)
    for d in range(1, n_col):
        to = lax.rem(c + d, n_col)
        send(remote(gfull.at[half, c], gfull.at[half, c], a_send.at[d], a_recv.at[c], (r, to)))

    for q in range(1, inner):
        at = lax.rem(lo + q, inner)
        remote(bparts.at[at], bparts.at[at], b_send.at[0], b_recv.at[at], (r, c)).wait_recv()
    bias_sum = bparts[0]
    for q in range(1, inner):
        bias_sum = bias_sum + bparts[q]
    bouter[hi] = bias_sum
    for d in range(1, outer):
        to = lax.rem(hi + d, outer)
        send(remote(bouter.at[hi], bouter.at[hi], d_send.at[d], d_recv.at[hi], (r, to * inner + lo)))
    own_sum = None
    for n, d in enumerate(order):
        if n % portion == 0:
            run, m = pl.ds(n, portion), n // portion
            for q in range(1, inner):
                at = lax.rem(b_at + q, inner)
                remote(ssend.at[at, run], srecv.at[at, run], s_send.at[0, 0], s_recv.at[m, at], (r, c)).wait_recv()
        part = ssend[b_at, n].astype(F32)
        for q in range(1, inner):
            part = part + srecv[lax.rem(b_at + q, inner), n].astype(F32)
        if d:
            to = lax.rem(a + d, outer)
            zsend[d] = part.astype(BF16)
            send(remote(zsend.at[d], zrecv.at[a], z_send.at[d], z_recv.at[a], (r, col_at(to, b_at))))
        else:
            own_sum = part
    sent()
    for d in range(1, outer):
        source = lax.rem(hi + d, outer)
        remote(bouter.at[source], bouter.at[source], d_send.at[0], d_recv.at[source], (r, c)).wait_recv()
    bias_sum = bouter[0]
    for k in range(1, outer):
        bias_sum = bias_sum + bouter[k]
    gb[...] = bias_sum
    stores = [store_h]

    def store(source, target, sem):
        copy = pltpu.make_async_copy(source, target, store_sem.at[sem])
        copy.start()
        stores.append(copy)

    store(gb, gb_out, 1)
    for d in range(1, n_col):
        source = lax.rem(c + d, n_col)
        remote(gfull.at[half, source], gfull.at[half, source], a_send.at[0], a_recv.at[source], (r, c)).wait_recv()
    if split == 2:
        partner = r + 1 - 2 * half
        send(remote(gfull.at[half], gfull.at[half], p_send.at[0], p_recv.at[0], (partner, c)))
    store(gfull.at[half], gw_out.at[half], 2)
    for d in nearest_first(outer):
        source = lax.rem(a + d, outer)
        remote(zsend.at[0], zrecv.at[source], z_send.at[0], z_recv.at[source], (r, c)).wait_recv()
        own_sum = own_sum + zrecv[source].astype(F32)
    gf[...] = own_sum.T.astype(BF16)
    store(gf, gf_out, 3)
    if split == 2:
        remote(gfull.at[1 - half], gfull.at[1 - half], p_send.at[0], p_recv.at[0], (r, c)).wait_recv()
        store(gfull.at[1 - half], gw_out.at[1 - half], 4)
    sent()
    for copy in stores:
        copy.wait()


def hand_over(hidden_in, gf_in, gw_in, gb_in, hidden_out, gf_out, gw_out, gb_out, hidden, gf, gw, wide, gb, load_sem, store_sem):
    chunk = gw.shape[3]
    parts = wide.shape[1] // chunk
    deep = wide.shape[0] // gw.shape[0]
    moves = (
        (gw_in, gw, wide, gw_out),
        (hidden_in, hidden, hidden, hidden_out),
        (gf_in, gf, gf, gf_out),
        (gb_in, gb, gb, gb_out),
    )
    loads = [pltpu.make_async_copy(moves[k][0], moves[k][1], load_sem.at[k]) for k in range(4)]
    stores = [pltpu.make_async_copy(moves[k][2], moves[k][3], store_sem.at[k]) for k in range(4)]
    for load in loads:
        load.start()
    for k in range(4):
        loads[k].wait()
        if k == 0:
            for n in range(gw.shape[0]):
                for m in range(gw.shape[1]):
                    top, l = n * deep + m // parts * GROUP, m % parts
                    wide[top : top + GROUP, l * chunk : (l + 1) * chunk] = gw[n, m].astype(F32)
        stores[k].start()
    for copy in stores:
        copy.wait()


def local(n_row, n_col, features, weight, bias, tile_values, tile_index, tile_count, cotangent):
    rows, feat = features.shape
    own_rows, width = cotangent.shape
    slots, size = tile_values.shape[2], tile_values.shape[3]
    inner = 4
    outer = n_col // inner
    target = n_row * own_rows
    source = n_col * rows
    chunk = feat * width // (GROUP * n_col)
    split = 2 if n_row % 2 == 0 and chunk % 256 == 0 else 1
    chunk = chunk // split
    dma = pltpu.SemaphoreType.DMA
    any_spec = pl.BlockSpec(memory_space=pl.ANY)
    hbm = pl.BlockSpec(memory_space=pltpu.HBM)
    hidden, gf, gw, gb = pl.pallas_call(
        functools.partial(kernel, n_row, n_col, inner, split),
        out_shape=(
            jax.ShapeDtypeStruct((own_rows, width), BF16),
            jax.ShapeDtypeStruct((rows, feat), BF16),
            jax.ShapeDtypeStruct((split, n_col, GROUP, chunk), BF16),
            jax.ShapeDtypeStruct((1, width), F32),
        ),
        in_specs=[hbm] * 5 + [pl.BlockSpec(memory_space=pltpu.SMEM), hbm],
        out_specs=(any_spec,) * 4,
        scratch_shapes=[
            pltpu.VMEM((source, feat), BF16),
            pltpu.VMEM((feat, width), BF16),
            pltpu.VMEM((1, width), F32),
            pltpu.VMEM((slots, size, size), BF16),
            pltpu.VMEM((target, source), BF16),
            pltpu.VMEM((n_row, own_rows, width), BF16),
            pltpu.VMEM((n_row, target, feat), F32),
            pltpu.VMEM((feat, target), BF16),
            pltpu.VMEM((n_row, own_rows, width), BF16),
            pltpu.VMEM((target, width), BF16),
            pltpu.VMEM((inner, outer, feat, rows), BF16),
            pltpu.VMEM((inner, outer, feat, rows), BF16),
            pltpu.VMEM((outer, feat, rows), BF16),
            pltpu.VMEM((outer, feat, rows), BF16),
            pltpu.VMEM((n_col, GROUP, chunk), BF16),
            pltpu.VMEM((n_col, GROUP, chunk), BF16),
            pltpu.VMEM((split, n_col, GROUP, chunk), BF16),
            pltpu.VMEM((inner, 1, width), F32),
            pltpu.VMEM((outer, 1, width), F32),
            pltpu.VMEM((1, width), F32),
            pltpu.VMEM((rows, feat), BF16),
            pltpu.SMEM(tile_index.shape, jnp.int32),
            dma((6,)), dma((5,)),
            dma((n_col,)), dma((n_col,)),
            dma((n_row,)), dma((n_row,)),
            dma((n_row,)), dma((n_row,)),
            dma((outer, inner)), dma((outer, inner)),
            dma((outer,)), dma((outer,)),
            dma((n_col,)), dma((n_col,)),
            dma((n_col,)), dma((n_col,)),
            dma((n_col,)), dma((n_col,)),
            dma((1,)), dma((1,)),
            dma((outer,)), dma((outer,)),
        ],
        compiler_params=pltpu.CompilerParams(
            collective_id=0, has_side_effects=True, vmem_limit_bytes=60 * 1024 * 1024
        ),
        cost_estimate=pl.CostEstimate(
            flops=4 * target * source * feat + 6 * target * width * feat,
            bytes_accessed=2 * (slots * size * size + 3 * own_rows * width),
            transcendentals=target * width,
        ),
    )(features, weight, bias.reshape(1, width), tile_values, tile_index, tile_count, cotangent)
    results = (hidden, gf, gw, gb)
    hidden, gf, gw, gb = pl.pallas_call(
        hand_over,
        out_shape=(
            jax.ShapeDtypeStruct(hidden.shape, BF16),
            jax.ShapeDtypeStruct(gf.shape, BF16),
            jax.ShapeDtypeStruct((feat, width), F32),
            jax.ShapeDtypeStruct(gb.shape, F32),
        ),
        in_specs=[any_spec] * 4,
        out_specs=(any_spec,) * 4,
        scratch_shapes=[
            pltpu.VMEM(hidden.shape, BF16),
            pltpu.VMEM(gf.shape, BF16),
            pltpu.VMEM(gw.shape, BF16),
            pltpu.VMEM((feat, width), F32),
            pltpu.VMEM(gb.shape, F32),
            dma((4,)),
            dma((4,)),
        ],
        compiler_params=pltpu.CompilerParams(vmem_limit_bytes=60 * 1024 * 1024),
    )(*results)
    return hidden, gf, gw, gb.reshape(width)


def solution(mesh):
    in_specs = (
        P(("row", "col"), None),
        P(),
        P(),
        P("row", "col", None, None, None),
        P("row", "col", None),
        P("row", "col"),
        P(("col", "row"), None),
    )
    out_specs = (P(("col", "row"), None), P(("row", "col"), None), P(), P())
    body = functools.partial(local, mesh.shape["row"], mesh.shape["col"])
    return jax.shard_map(body, mesh=mesh, in_specs=in_specs, out_specs=out_specs, check_vma=False)
```

```python
import functools

import jax
import jax.numpy as jnp
from jax import lax
from jax.experimental import pallas as pl
from jax.experimental.pallas import tpu as pltpu
from jax.sharding import PartitionSpec as P

MESH = pl.DeviceIdType.MESH
F32 = jnp.float32
BF16 = jnp.bfloat16
GROUP = 16


def nearest_first(count):
    return sorted(range(1, count), key=lambda d: (min(d, count - d), d))


def remote(src, dst, send, recv, device):
    return pltpu.make_async_remote_copy(
        src_ref=src, dst_ref=dst, send_sem=send, recv_sem=recv, device_id=device, device_id_type=MESH
    )


def kernel(
    n_row, n_col, inner,
    features, weight, bias, tiles_in, index_in, count, cotangent,
    hidden_out, gf_out, gw_out, gb_out,
    x, w, b, tiles, adj, cot, hpart, hts, hid, dpre,
    ssend, srecv, zsend, zrecv, gsend, grecv, gmid, gouter, gfull, bparts, bouter, gb, gf, index,
    load_sem, store_sem, x_send, x_recv, c_send, c_recv, h_send, h_recv,
    s_send, s_recv, z_send, z_recv, g_send, g_recv, m_send, m_recv, a_send, a_recv, b_send, b_recv, p_send, p_recv, d_send, d_recv,
):
    r = lax.axis_index("row")
    c = lax.axis_index("col")
    outer = n_col // inner
    hi = c // inner
    lo = lax.rem(c, inner)
    swap = lax.rem(r, 2) if outer == inner else 0
    a = hi + swap * (lo - hi)
    b_at = lo + swap * (hi - lo)

    def col_at(first, second):
        return (first + swap * (second - first)) * inner + second + swap * (first - second)

    def place_of(col):
        high, low = col // inner, lax.rem(col, inner)
        return (high + swap * (low - high)) * inner + low + swap * (high - low)

    me = a * inner + b_at
    rows = features.shape[0]
    own_rows = cot.shape[1]
    width = w.shape[1]
    slots, size = tiles.shape[0], tiles.shape[1]
    tile_cols = n_col * rows // size
    tile_rows = n_row * own_rows // size

    def block(spot):
        return pl.ds(pl.multiple_of(spot * rows, rows), rows)

    def turned(turn_a, turn_b):
        return lax.rem(a + turn_a, outer), lax.rem(b_at + turn_b, inner)

    def spot_of(turn_a, turn_b):
        first, second = turned(turn_a, turn_b)
        return first * inner + second

    def col_of(turn_a, turn_b):
        return col_at(*turned(turn_a, turn_b))

    load_x = pltpu.make_async_copy(features, x.at[block(me)], load_sem.at[0])
    load_c = pltpu.make_async_copy(cotangent, cot.at[r], load_sem.at[1])
    load_t = pltpu.make_async_copy(tiles_in.at[0, 0], tiles, load_sem.at[2])
    load_w = pltpu.make_async_copy(weight, w, load_sem.at[3])
    load_b = pltpu.make_async_copy(bias, b, load_sem.at[4])
    load_i = pltpu.make_async_copy(index_in, index, load_sem.at[5])
    for load in (load_x, load_c, load_t, load_w, load_b, load_i):
        load.start()

    barrier = pltpu.get_barrier_semaphore()
    for d in range(1, outer):
        pl.semaphore_signal(barrier, inc=1, device_id=(r, col_of(d, 0)), device_id_type=MESH)
    for q in range(1, inner):
        pl.semaphore_signal(barrier, inc=1, device_id=(r, col_of(0, q)), device_id_type=MESH)
    for d in range(1, n_row):
        pl.semaphore_signal(barrier, inc=1, device_id=(lax.rem(r + d, n_row), c), device_id_type=MESH)
    pl.semaphore_wait(barrier, outer + inner + n_row - 3)

    pending = []

    def send(copy):
        copy.start()
        pending.append(copy)

    def sent():
        for copy in pending:
            copy.wait_send()
        pending.clear()

    def send_x(number, source, to):
        send(remote(x.at[block(source)], x.at[block(source)], x_send.at[number], x_recv.at[source], (r, to)))

    def wait_x(source):
        remote(x.at[block(source)], x.at[block(source)], x_send.at[0], x_recv.at[source], (r, c)).wait_recv()

    number = 0
    load_x.wait()
    for d in nearest_first(outer):
        send_x(number, me, col_of(d, 0))
        number += 1
    for q in range(1, inner):
        send_x(number, me, col_of(0, q))
        number += 1
    load_c.wait()
    for d in range(1, n_row):
        send(remote(cot.at[r], cot.at[r], c_send.at[d], c_recv.at[r], (lax.rem(r + d, n_row), c)))

    load_t.wait()
    load_i.wait()
    live = count[0, 0]

    def place(t, carry):
        def find(s, slot):
            return jnp.where((index[0, 0, s] == t) & (s < live), s, slot)

        slot = lax.fori_loop(0, slots, find, jnp.int32(-1), unroll=min(slots, 16))
        tile = tiles[jnp.maximum(slot, 0)]
        row = pl.ds(pl.multiple_of(t // tile_cols * size, size), size)
        column = pl.ds(pl.multiple_of(place_of(lax.rem(t, tile_cols)) * size, size), size)
        adj[row, column] = jnp.where(slot >= 0, tile, jnp.zeros_like(tile))
        return carry

    places = tile_rows * tile_cols
    piece = places // outer
    for m, d in enumerate(nearest_first(outer)):
        lax.fori_loop(m * piece, (m + 1) * piece, place, 0)
        source = spot_of(d, 0)
        wait_x(source)
        for q in range(1, inner):
            send_x(number, source, col_of(0, q))
            number += 1
    lax.fori_loop((outer - 1) * piece, places, place, 0)
    span = inner * rows
    partial = None
    for d in [0] + nearest_first(outer):
        for q in range(1, inner):
            wait_x(spot_of(d, q))
        group = pl.ds(pl.multiple_of(lax.rem(a + d, outer) * span, span), span)
        part = jnp.dot(adj[:, group], x[group, :], preferred_element_type=F32)
        partial = part if partial is None else partial + part
    hpart[r] = partial
    for d in range(1, n_row):
        send(remote(hpart.at[r], hpart.at[r], h_send.at[d], h_recv.at[r], (lax.rem(r + d, n_row), c)))
    load_w.wait()
    load_b.wait()
    for d in range(1, n_row):
        other = lax.rem(r + d, n_row)
        remote(cot.at[other], cot.at[other], c_send.at[0], c_recv.at[other], (r, c)).wait_recv()
    for d in range(1, n_row):
        other = lax.rem(r + d, n_row)
        remote(hpart.at[other], hpart.at[other], h_send.at[0], h_recv.at[other], (r, c)).wait_recv()
    h = hpart[0]
    for k in range(1, n_row):
        h = h + hpart[k]
    hb = h.astype(BF16)
    hts[...] = h.T.astype(BF16)

    bias_sum = jnp.zeros((1, width), F32)
    for k in range(n_row):
        part = hb[k * own_rows : (k + 1) * own_rows]
        pre = jnp.dot(part, w[...], preferred_element_type=F32) + b[...]
        sig = 0.5 * jnp.tanh(0.5 * pre) + 0.5
        hid[k] = (pre * sig).astype(BF16)
        grad = (cot[k].astype(F32) * (sig + pre * sig * (1.0 - sig))).astype(BF16)
        dpre[k * own_rows : (k + 1) * own_rows, :] = grad
        bias_sum = bias_sum + jnp.sum(grad.astype(F32), axis=0, keepdims=True)
    store_h = pltpu.make_async_copy(hid.at[r], hidden_out, store_sem.at[0])
    store_h.start()

    gw = jnp.dot(hts[...], dpre[...], preferred_element_type=F32).astype(BF16)
    chunk = gsend.shape[3]
    parts = width // chunk
    for k in range(n_col):
        g, l = k // parts, k % parts
        gsend[k // outer, k % outer] = gw[g * GROUP : (g + 1) * GROUP, l * chunk : (l + 1) * chunk]
    for q in range(1, inner):
        at = lax.rem(lo + q, inner)
        send(remote(gsend.at[at], grecv.at[lo], g_send.at[q], g_recv.at[lo], (r, hi * inner + at)))
    grecv[lo] = gsend[lo]

    gt = lax.dot_general(w[...], dpre[...], (((1,), (1,)), ((), ())), preferred_element_type=F32).astype(BF16)
    order = nearest_first(outer) + [0]
    portion = max(1, outer // 2)
    for n, d in enumerate(order):
        columns = pl.ds(pl.multiple_of(lax.rem(a + d, outer) * span, span), span)
        part = jnp.dot(gt, adj[:, columns], preferred_element_type=F32).astype(BF16)
        for q in range(inner):
            ssend[q, n] = part[:, q * rows : (q + 1) * rows]
        if (n + 1) % portion == 0:
            run, m = pl.ds(n + 1 - portion, portion), n // portion
            for q in range(1, inner):
                at = lax.rem(b_at + q, inner)
                send(remote(ssend.at[at, run], srecv.at[b_at, run], s_send.at[m, q], s_recv.at[m, b_at], (r, col_at(a, at))))
    bparts[lo] = bias_sum
    for q in range(1, inner):
        at = lax.rem(lo + q, inner)
        send(remote(bparts.at[lo], bparts.at[lo], b_send.at[q], b_recv.at[lo], (r, hi * inner + at)))

    for q in range(1, inner):
        at = lax.rem(lo + q, inner)
        remote(gsend.at[0], grecv.at[at], g_send.at[0], g_recv.at[at], (r, c)).wait_recv()
    total = grecv[0].astype(F32)
    for k in range(1, inner):
        total = total + grecv[k].astype(F32)
    gmid[...] = total.astype(BF16)
    for d in range(1, outer):
        to = lax.rem(hi + d, outer)
        send(remote(gmid.at[to], gouter.at[hi], m_send.at[d], m_recv.at[hi], (r, to * inner + lo)))
    gouter[hi] = gmid[hi]

    def pass_on(n, d):
        if n % portion == 0:
            run, m = pl.ds(n, portion), n // portion
            for q in range(1, inner):
                at = lax.rem(b_at + q, inner)
                remote(ssend.at[at, run], srecv.at[at, run], s_send.at[0, 0], s_recv.at[m, at], (r, c)).wait_recv()
        part = ssend[b_at, n].astype(F32)
        for q in range(1, inner):
            part = part + srecv[lax.rem(b_at + q, inner), n].astype(F32)
        if d:
            zsend[d] = part.astype(BF16)
            to = col_at(lax.rem(a + d, outer), b_at)
            send(remote(zsend.at[d], zrecv.at[a], z_send.at[d], z_recv.at[a], (r, to)))
        return part

    for n in range(portion):
        pass_on(n, order[n])
    for d in range(1, outer):
        source = lax.rem(hi + d, outer)
        remote(gmid.at[0], gouter.at[source], m_send.at[0], m_recv.at[source], (r, c)).wait_recv()
    total = gouter[0].astype(F32)
    for k in range(1, outer):
        total = total + gouter[k].astype(F32)
    gfull[lo, hi] = total.astype(BF16)
    for d in range(1, outer):
        to = lax.rem(hi + d, outer)
        send(remote(gfull.at[lo, hi], gfull.at[lo, hi], a_send.at[d], a_recv.at[hi], (r, to * inner + lo)))
    for n in range(portion, outer):
        own_sum = pass_on(n, order[n])
    for q in range(1, inner):
        at = lax.rem(lo + q, inner)
        remote(bparts.at[at], bparts.at[at], b_send.at[0], b_recv.at[at], (r, c)).wait_recv()
    bias_sum = bparts[0]
    for q in range(1, inner):
        bias_sum = bias_sum + bparts[q]
    bouter[hi] = bias_sum
    for d in range(1, outer):
        to = lax.rem(hi + d, outer)
        send(remote(bouter.at[hi], bouter.at[hi], d_send.at[d], d_recv.at[hi], (r, to * inner + lo)))
    for d in range(1, outer):
        source = lax.rem(hi + d, outer)
        remote(gfull.at[lo, source], gfull.at[lo, source], a_send.at[0], a_recv.at[source], (r, c)).wait_recv()
    for q in range(1, inner):
        at = lax.rem(lo + q, inner)
        send(remote(gfull.at[lo], gfull.at[lo], p_send.at[q], p_recv.at[lo], (r, hi * inner + at)))
    for d in range(1, outer):
        source = lax.rem(hi + d, outer)
        remote(bouter.at[source], bouter.at[source], d_send.at[0], d_recv.at[source], (r, c)).wait_recv()
    bias_sum = bouter[0]
    for k in range(1, outer):
        bias_sum = bias_sum + bouter[k]
    gb[...] = bias_sum
    stores = [store_h]

    def store(source, target, sem):
        copy = pltpu.make_async_copy(source, target, store_sem.at[sem])
        copy.start()
        stores.append(copy)

    store(gb, gb_out, 1)
    for d in nearest_first(outer):
        source = lax.rem(a + d, outer)
        remote(zsend.at[0], zrecv.at[source], z_send.at[0], z_recv.at[source], (r, c)).wait_recv()
        own_sum = own_sum + zrecv[source].astype(F32)
    gf[...] = own_sum.T.astype(BF16)
    store(gf, gf_out, 2)
    sent()
    for q in range(1, inner):
        at = lax.rem(lo + q, inner)
        remote(gfull.at[at], gfull.at[at], p_send.at[0], p_recv.at[at], (r, c)).wait_recv()
    store(gfull, gw_out, 3)
    for copy in stores:
        copy.wait()


def hand_over(hidden_in, gf_in, gw_in, gb_in, hidden_out, gf_out, gw_out, gb_out, hidden, gf, gw, wide, gb, load_sem, store_sem):
    chunk = gw.shape[3]
    parts = wide.shape[1] // chunk
    moves = (
        (gw_in, gw, wide, gw_out),
        (hidden_in, hidden, hidden, hidden_out),
        (gf_in, gf, gf, gf_out),
        (gb_in, gb, gb, gb_out),
    )
    loads = [pltpu.make_async_copy(moves[k][0], moves[k][1], load_sem.at[k]) for k in range(4)]
    stores = [pltpu.make_async_copy(moves[k][2], moves[k][3], store_sem.at[k]) for k in range(4)]
    for load in loads:
        load.start()
    for k in range(4):
        loads[k].wait()
        if k == 0:
            for n in range(gw.shape[0]):
                for m in range(gw.shape[1]):
                    number = n * gw.shape[1] + m
                    top, l = number // parts * GROUP, number % parts
                    wide[top : top + GROUP, l * chunk : (l + 1) * chunk] = gw[n, m].astype(F32)
        stores[k].start()
    for copy in stores:
        copy.wait()


def local(n_row, n_col, features, weight, bias, tile_values, tile_index, tile_count, cotangent):
    rows, feat = features.shape
    own_rows, width = cotangent.shape
    slots, size = tile_values.shape[2], tile_values.shape[3]
    inner = 4
    outer = n_col // inner
    target = n_row * own_rows
    source = n_col * rows
    chunk = feat * width // (GROUP * n_col)
    dma = pltpu.SemaphoreType.DMA
    any_spec = pl.BlockSpec(memory_space=pl.ANY)
    hbm = pl.BlockSpec(memory_space=pltpu.HBM)
    hidden, gf, gw, gb = pl.pallas_call(
        functools.partial(kernel, n_row, n_col, inner),
        out_shape=(
            jax.ShapeDtypeStruct((own_rows, width), BF16),
            jax.ShapeDtypeStruct((rows, feat), BF16),
            jax.ShapeDtypeStruct((inner, outer, GROUP, chunk), BF16),
            jax.ShapeDtypeStruct((1, width), F32),
        ),
        in_specs=[hbm] * 5 + [pl.BlockSpec(memory_space=pltpu.SMEM), hbm],
        out_specs=(any_spec,) * 4,
        scratch_shapes=[
            pltpu.VMEM((source, feat), BF16),
            pltpu.VMEM((feat, width), BF16),
            pltpu.VMEM((1, width), F32),
            pltpu.VMEM((slots, size, size), BF16),
            pltpu.VMEM((target, source), BF16),
            pltpu.VMEM((n_row, own_rows, width), BF16),
            pltpu.VMEM((n_row, target, feat), F32),
            pltpu.VMEM((feat, target), BF16),
            pltpu.VMEM((n_row, own_rows, width), BF16),
            pltpu.VMEM((target, width), BF16),
            pltpu.VMEM((inner, outer, feat, rows), BF16),
            pltpu.VMEM((inner, outer, feat, rows), BF16),
            pltpu.VMEM((outer, feat, rows), BF16),
            pltpu.VMEM((outer, feat, rows), BF16),
            pltpu.VMEM((inner, outer, GROUP, chunk), BF16),
            pltpu.VMEM((inner, outer, GROUP, chunk), BF16),
            pltpu.VMEM((outer, GROUP, chunk), BF16),
            pltpu.VMEM((outer, GROUP, chunk), BF16),
            pltpu.VMEM((inner, outer, GROUP, chunk), BF16),
            pltpu.VMEM((inner, 1, width), F32),
            pltpu.VMEM((outer, 1, width), F32),
            pltpu.VMEM((1, width), F32),
            pltpu.VMEM((rows, feat), BF16),
            pltpu.SMEM(tile_index.shape, jnp.int32),
            dma((6,)), dma((4,)),
            dma((n_col,)), dma((n_col,)),
            dma((n_row,)), dma((n_row,)),
            dma((n_row,)), dma((n_row,)),
            dma((outer, inner)), dma((outer, inner)),
            dma((outer,)), dma((outer,)),
            dma((inner,)), dma((inner,)),
            dma((outer,)), dma((outer,)),
            dma((outer,)), dma((outer,)),
            dma((inner,)), dma((inner,)),
            dma((inner,)), dma((inner,)),
            dma((outer,)), dma((outer,)),
        ],
        compiler_params=pltpu.CompilerParams(
            collective_id=0, has_side_effects=True, vmem_limit_bytes=60 * 1024 * 1024
        ),
        cost_estimate=pl.CostEstimate(
            flops=4 * target * source * feat + 6 * target * width * feat,
            bytes_accessed=2 * (slots * size * size + 3 * own_rows * width),
            transcendentals=target * width,
        ),
    )(features, weight, bias.reshape(1, width), tile_values, tile_index, tile_count, cotangent)
    results = (hidden, gf, gw, gb)
    hidden, gf, gw, gb = pl.pallas_call(
        hand_over,
        out_shape=(
            jax.ShapeDtypeStruct(hidden.shape, BF16),
            jax.ShapeDtypeStruct(gf.shape, BF16),
            jax.ShapeDtypeStruct((feat, width), F32),
            jax.ShapeDtypeStruct(gb.shape, F32),
        ),
        in_specs=[any_spec] * 4,
        out_specs=(any_spec,) * 4,
        scratch_shapes=[
            pltpu.VMEM(hidden.shape, BF16),
            pltpu.VMEM(gf.shape, BF16),
            pltpu.VMEM(gw.shape, BF16),
            pltpu.VMEM((feat, width), F32),
            pltpu.VMEM(gb.shape, F32),
            dma((4,)),
            dma((4,)),
        ],
        compiler_params=pltpu.CompilerParams(vmem_limit_bytes=60 * 1024 * 1024),
    )(*results)
    return hidden, gf, gw, gb.reshape(width)


def solution(mesh):
    in_specs = (
        P(("row", "col"), None),
        P(),
        P(),
        P("row", "col", None, None, None),
        P("row", "col", None),
        P("row", "col"),
        P(("col", "row"), None),
    )
    out_specs = (P(("col", "row"), None), P(("row", "col"), None), P(), P())
    body = functools.partial(local, mesh.shape["row"], mesh.shape["col"])
    return jax.shard_map(body, mesh=mesh, in_specs=in_specs, out_specs=out_specs, check_vma=False)
```

```python
import functools

import jax
import jax.numpy as jnp
from jax import lax
from jax.experimental import pallas as pl
from jax.experimental.pallas import tpu as pltpu
from jax.sharding import PartitionSpec as P

MESH = pl.DeviceIdType.MESH
F32 = jnp.float32
BF16 = jnp.bfloat16
GROUP = 16


def nearest_first(count):
    return sorted(range(1, count), key=lambda d: (min(d, count - d), d))


def remote(src, dst, send, recv, device):
    return pltpu.make_async_remote_copy(
        src_ref=src, dst_ref=dst, send_sem=send, recv_sem=recv, device_id=device, device_id_type=MESH
    )


def kernel(
    n_row, n_col, inner, split,
    features, weight, bias, tiles_in, index_in, count, cotangent,
    hidden_out, gf_out, gw_out, gb_out,
    x, w, b, tiles, adj, cot, hpart, hts, hid, dpre,
    ssend, srecv, zsend, zrecv, gsend, grecv, gfull, bparts, bouter, gb, gf, index,
    load_sem, store_sem, x_send, x_recv, c_send, c_recv, h_send, h_recv,
    s_send, s_recv, z_send, z_recv, g_send, g_recv, a_send, a_recv, b_send, b_recv, p_send, p_recv, d_send, d_recv,
):
    r = lax.axis_index("row")
    c = lax.axis_index("col")
    outer = n_col // inner
    hi = c // inner
    lo = lax.rem(c, inner)
    swap = lax.rem(r, 2) if outer == inner else 0
    a = hi + swap * (lo - hi)
    b_at = lo + swap * (hi - lo)

    def col_at(first, second):
        return (first + swap * (second - first)) * inner + second + swap * (first - second)

    def place_of(col):
        high, low = col // inner, lax.rem(col, inner)
        return (high + swap * (low - high)) * inner + low + swap * (high - low)

    me = a * inner + b_at
    rows = features.shape[0]
    own_rows = cot.shape[1]
    width = w.shape[1]
    slots, size = tiles.shape[0], tiles.shape[1]
    tile_cols = n_col * rows // size
    tile_rows = n_row * own_rows // size

    def block(spot):
        return pl.ds(pl.multiple_of(spot * rows, rows), rows)

    def turned(turn_a, turn_b):
        return lax.rem(a + turn_a, outer), lax.rem(b_at + turn_b, inner)

    def spot_of(turn_a, turn_b):
        first, second = turned(turn_a, turn_b)
        return first * inner + second

    def col_of(turn_a, turn_b):
        return col_at(*turned(turn_a, turn_b))

    load_x = pltpu.make_async_copy(features, x.at[block(me)], load_sem.at[0])
    load_c = pltpu.make_async_copy(cotangent, cot.at[r], load_sem.at[1])
    load_t = pltpu.make_async_copy(tiles_in.at[0, 0], tiles, load_sem.at[2])
    load_w = pltpu.make_async_copy(weight, w, load_sem.at[3])
    load_b = pltpu.make_async_copy(bias, b, load_sem.at[4])
    load_i = pltpu.make_async_copy(index_in, index, load_sem.at[5])
    for load in (load_x, load_c, load_t, load_w, load_b, load_i):
        load.start()

    barrier = pltpu.get_barrier_semaphore()
    for d in range(1, n_col):
        pl.semaphore_signal(barrier, inc=1, device_id=(r, lax.rem(c + d, n_col)), device_id_type=MESH)
    for d in range(1, n_row):
        pl.semaphore_signal(barrier, inc=1, device_id=(lax.rem(r + d, n_row), c), device_id_type=MESH)
    pl.semaphore_wait(barrier, n_col + n_row - 2)

    pending = []

    def send(copy):
        copy.start()
        pending.append(copy)

    def sent():
        for copy in pending:
            copy.wait_send()
        pending.clear()

    def send_x(number, source, to):
        send(remote(x.at[block(source)], x.at[block(source)], x_send.at[number], x_recv.at[source], (r, to)))

    def wait_x(source):
        remote(x.at[block(source)], x.at[block(source)], x_send.at[0], x_recv.at[source], (r, c)).wait_recv()

    number = 0
    load_x.wait()
    for d in nearest_first(outer):
        send_x(number, me, col_of(d, 0))
        number += 1
    for q in range(1, inner):
        send_x(number, me, col_of(0, q))
        number += 1
    load_c.wait()
    for d in range(1, n_row):
        send(remote(cot.at[r], cot.at[r], c_send.at[d], c_recv.at[r], (lax.rem(r + d, n_row), c)))

    load_t.wait()
    load_i.wait()
    live = count[0, 0]

    def place(t, carry):
        def find(s, slot):
            return jnp.where((index[0, 0, s] == t) & (s < live), s, slot)

        slot = lax.fori_loop(0, slots, find, jnp.int32(-1), unroll=min(slots, 16))
        tile = tiles[jnp.maximum(slot, 0)]
        row = pl.ds(pl.multiple_of(t // tile_cols * size, size), size)
        column = pl.ds(pl.multiple_of(place_of(lax.rem(t, tile_cols)) * size, size), size)
        adj[row, column] = jnp.where(slot >= 0, tile, jnp.zeros_like(tile))
        return carry

    places = tile_rows * tile_cols
    piece = places // outer
    for m, d in enumerate(nearest_first(outer)):
        lax.fori_loop(m * piece, (m + 1) * piece, place, 0)
        source = spot_of(d, 0)
        wait_x(source)
        for q in range(1, inner):
            send_x(number, source, col_of(0, q))
            number += 1
    lax.fori_loop((outer - 1) * piece, places, place, 0)
    span = inner * rows
    partial = None
    for d in [0] + nearest_first(outer):
        for q in range(1, inner):
            wait_x(spot_of(d, q))
        group = pl.ds(pl.multiple_of(lax.rem(a + d, outer) * span, span), span)
        part = jnp.dot(adj[:, group], x[group, :], preferred_element_type=F32)
        partial = part if partial is None else partial + part
    hpart[r] = partial
    for d in range(1, n_row):
        send(remote(hpart.at[r], hpart.at[r], h_send.at[d], h_recv.at[r], (lax.rem(r + d, n_row), c)))
    load_w.wait()
    load_b.wait()
    for d in range(1, n_row):
        other = lax.rem(r + d, n_row)
        remote(cot.at[other], cot.at[other], c_send.at[0], c_recv.at[other], (r, c)).wait_recv()
    for d in range(1, n_row):
        other = lax.rem(r + d, n_row)
        remote(hpart.at[other], hpart.at[other], h_send.at[0], h_recv.at[other], (r, c)).wait_recv()
    h = hpart[0]
    for k in range(1, n_row):
        h = h + hpart[k]
    hb = h.astype(BF16)
    hts[...] = h.T.astype(BF16)

    for k in range(n_row):
        part = hb[k * own_rows : (k + 1) * own_rows]
        pre = jnp.dot(part, w[...], preferred_element_type=F32) + b[...]
        sig = 0.5 * jnp.tanh(0.5 * pre) + 0.5
        hid[k] = (pre * sig).astype(BF16)
        grad = (cot[k].astype(F32) * (sig + pre * sig * (1.0 - sig))).astype(BF16)
        dpre[k * own_rows : (k + 1) * own_rows, :] = grad
    store_h = pltpu.make_async_copy(hid.at[r], hidden_out, store_sem.at[0])
    store_h.start()

    half = lax.rem(r, split)
    deep = hts.shape[0] // split
    gw = jnp.dot(hts[pl.ds(pl.multiple_of(half * deep, deep), deep), :], dpre[...], preferred_element_type=F32).astype(BF16)
    chunk = gsend.shape[2]
    parts = width // chunk
    for k in range(n_col):
        g, l = k // parts, k % parts
        gsend[k] = gw[g * GROUP : (g + 1) * GROUP, l * chunk : (l + 1) * chunk]
    grecv[c] = gsend[c]
    for d in range(1, n_col):
        to = lax.rem(c + d, n_col)
        send(remote(gsend.at[to], grecv.at[c], g_send.at[d], g_recv.at[c], (r, to)))

    gt = lax.dot_general(w[...], dpre[...], (((1,), (1,)), ((), ())), preferred_element_type=F32).astype(BF16)
    order = nearest_first(outer) + [0]
    portion = max(1, outer // 2)
    for n, d in enumerate(order):
        columns = pl.ds(pl.multiple_of(lax.rem(a + d, outer) * span, span), span)
        part = jnp.dot(gt, adj[:, columns], preferred_element_type=F32).astype(BF16)
        for q in range(inner):
            ssend[q, n] = part[:, q * rows : (q + 1) * rows]
        if (n + 1) % portion == 0:
            run, m = pl.ds(n + 1 - portion, portion), n // portion
            for q in range(1, inner):
                at = lax.rem(b_at + q, inner)
                send(remote(ssend.at[at, run], srecv.at[b_at, run], s_send.at[m, q], s_recv.at[m, b_at], (r, col_at(a, at))))
    bparts[lo] = jnp.sum(dpre[...].astype(F32), axis=0, keepdims=True)
    for q in range(1, inner):
        at = lax.rem(lo + q, inner)
        send(remote(bparts.at[lo], bparts.at[lo], b_send.at[q], b_recv.at[lo], (r, hi * inner + at)))

    for d in range(1, n_col):
        source = lax.rem(c + d, n_col)
        remote(gsend.at[0], grecv.at[source], g_send.at[0], g_recv.at[source], (r, c)).wait_recv()
    total = grecv[0].astype(F32)
    for k in range(1, n_col):
        total = total + grecv[k].astype(F32)
    gfull[half, c] = total.astype(BF16)
    for d in range(1, n_col):
        to = lax.rem(c + d, n_col)
        send(remote(gfull.at[half, c], gfull.at[half, c], a_send.at[d], a_recv.at[c], (r, to)))

    for q in range(1, inner):
        at = lax.rem(lo + q, inner)
        remote(bparts.at[at], bparts.at[at], b_send.at[0], b_recv.at[at], (r, c)).wait_recv()
    bias_sum = bparts[0]
    for q in range(1, inner):
        bias_sum = bias_sum + bparts[q]
    bouter[hi] = bias_sum
    for d in range(1, outer):
        to = lax.rem(hi + d, outer)
        send(remote(bouter.at[hi], bouter.at[hi], d_send.at[d], d_recv.at[hi], (r, to * inner + lo)))
    own_sum = None
    for n, d in enumerate(order):
        if n % portion == 0:
            run, m = pl.ds(n, portion), n // portion
            for q in range(1, inner):
                at = lax.rem(b_at + q, inner)
                remote(ssend.at[at, run], srecv.at[at, run], s_send.at[0, 0], s_recv.at[m, at], (r, c)).wait_recv()
        part = ssend[b_at, n].astype(F32)
        for q in range(1, inner):
            part = part + srecv[lax.rem(b_at + q, inner), n].astype(F32)
        if d:
            to = lax.rem(a + d, outer)
            zsend[d] = part.astype(BF16)
            send(remote(zsend.at[d], zrecv.at[a], z_send.at[d], z_recv.at[a], (r, col_at(to, b_at))))
        else:
            own_sum = part
    sent()
    for d in range(1, outer):
        source = lax.rem(hi + d, outer)
        remote(bouter.at[source], bouter.at[source], d_send.at[0], d_recv.at[source], (r, c)).wait_recv()
    bias_sum = bouter[0]
    for k in range(1, outer):
        bias_sum = bias_sum + bouter[k]
    gb[...] = bias_sum
    stores = [store_h]

    def store(source, target, sem):
        copy = pltpu.make_async_copy(source, target, store_sem.at[sem])
        copy.start()
        stores.append(copy)

    store(gb, gb_out, 1)
    for d in range(1, n_col):
        source = lax.rem(c + d, n_col)
        remote(gfull.at[half, source], gfull.at[half, source], a_send.at[0], a_recv.at[source], (r, c)).wait_recv()
    if split == 2:
        partner = r + 1 - 2 * half
        send(remote(gfull.at[half], gfull.at[half], p_send.at[0], p_recv.at[0], (partner, c)))
    store(gfull.at[half], gw_out.at[half], 2)
    for d in nearest_first(outer):
        source = lax.rem(a + d, outer)
        remote(zsend.at[0], zrecv.at[source], z_send.at[0], z_recv.at[source], (r, c)).wait_recv()
        own_sum = own_sum + zrecv[source].astype(F32)
    gf[...] = own_sum.T.astype(BF16)
    store(gf, gf_out, 3)
    if split == 2:
        remote(gfull.at[1 - half], gfull.at[1 - half], p_send.at[0], p_recv.at[0], (r, c)).wait_recv()
        store(gfull.at[1 - half], gw_out.at[1 - half], 4)
    sent()
    for copy in stores:
        copy.wait()


def hand_over(hidden_in, gf_in, gw_in, gb_in, hidden_out, gf_out, gw_out, gb_out, hidden, gf, gw, wide, gb, load_sem, store_sem):
    chunk = gw.shape[3]
    parts = wide.shape[1] // chunk
    deep = wide.shape[0] // gw.shape[0]
    moves = (
        (gw_in, gw, wide, gw_out),
        (hidden_in, hidden, hidden, hidden_out),
        (gf_in, gf, gf, gf_out),
        (gb_in, gb, gb, gb_out),
    )
    loads = [pltpu.make_async_copy(moves[k][0], moves[k][1], load_sem.at[k]) for k in range(4)]
    stores = [pltpu.make_async_copy(moves[k][2], moves[k][3], store_sem.at[k]) for k in range(4)]
    for load in loads:
        load.start()
    for k in range(4):
        loads[k].wait()
        if k == 0:
            for n in range(gw.shape[0]):
                for m in range(gw.shape[1]):
                    top, l = n * deep + m // parts * GROUP, m % parts
                    wide[top : top + GROUP, l * chunk : (l + 1) * chunk] = gw[n, m].astype(F32)
        stores[k].start()
    for copy in stores:
        copy.wait()


def local(n_row, n_col, features, weight, bias, tile_values, tile_index, tile_count, cotangent):
    rows, feat = features.shape
    own_rows, width = cotangent.shape
    slots, size = tile_values.shape[2], tile_values.shape[3]
    inner = 4
    outer = n_col // inner
    target = n_row * own_rows
    source = n_col * rows
    chunk = feat * width // (GROUP * n_col)
    split = 2 if n_row % 2 == 0 and chunk % 256 == 0 else 1
    chunk = chunk // split
    dma = pltpu.SemaphoreType.DMA
    any_spec = pl.BlockSpec(memory_space=pl.ANY)
    hbm = pl.BlockSpec(memory_space=pltpu.HBM)
    hidden, gf, gw, gb = pl.pallas_call(
        functools.partial(kernel, n_row, n_col, inner, split),
        out_shape=(
            jax.ShapeDtypeStruct((own_rows, width), BF16),
            jax.ShapeDtypeStruct((rows, feat), BF16),
            jax.ShapeDtypeStruct((split, n_col, GROUP, chunk), BF16),
            jax.ShapeDtypeStruct((1, width), F32),
        ),
        in_specs=[hbm] * 5 + [pl.BlockSpec(memory_space=pltpu.SMEM), hbm],
        out_specs=(any_spec,) * 4,
        scratch_shapes=[
            pltpu.VMEM((source, feat), BF16),
            pltpu.VMEM((feat, width), BF16),
            pltpu.VMEM((1, width), F32),
            pltpu.VMEM((slots, size, size), BF16),
            pltpu.VMEM((target, source), BF16),
            pltpu.VMEM((n_row, own_rows, width), BF16),
            pltpu.VMEM((n_row, target, feat), F32),
            pltpu.VMEM((feat, target), BF16),
            pltpu.VMEM((n_row, own_rows, width), BF16),
            pltpu.VMEM((target, width), BF16),
            pltpu.VMEM((inner, outer, feat, rows), BF16),
            pltpu.VMEM((inner, outer, feat, rows), BF16),
            pltpu.VMEM((outer, feat, rows), BF16),
            pltpu.VMEM((outer, feat, rows), BF16),
            pltpu.VMEM((n_col, GROUP, chunk), BF16),
            pltpu.VMEM((n_col, GROUP, chunk), BF16),
            pltpu.VMEM((split, n_col, GROUP, chunk), BF16),
            pltpu.VMEM((inner, 1, width), F32),
            pltpu.VMEM((outer, 1, width), F32),
            pltpu.VMEM((1, width), F32),
            pltpu.VMEM((rows, feat), BF16),
            pltpu.SMEM(tile_index.shape, jnp.int32),
            dma((6,)), dma((5,)),
            dma((n_col,)), dma((n_col,)),
            dma((n_row,)), dma((n_row,)),
            dma((n_row,)), dma((n_row,)),
            dma((outer, inner)), dma((outer, inner)),
            dma((outer,)), dma((outer,)),
            dma((n_col,)), dma((n_col,)),
            dma((n_col,)), dma((n_col,)),
            dma((n_col,)), dma((n_col,)),
            dma((1,)), dma((1,)),
            dma((outer,)), dma((outer,)),
        ],
        compiler_params=pltpu.CompilerParams(
            collective_id=0, has_side_effects=True, vmem_limit_bytes=60 * 1024 * 1024
        ),
        cost_estimate=pl.CostEstimate(
            flops=4 * target * source * feat + 6 * target * width * feat,
            bytes_accessed=2 * (slots * size * size + 3 * own_rows * width),
            transcendentals=target * width,
        ),
    )(features, weight, bias.reshape(1, width), tile_values, tile_index, tile_count, cotangent)
    results = (hidden, gf, gw, gb)
    hidden, gf, gw, gb = pl.pallas_call(
        hand_over,
        out_shape=(
            jax.ShapeDtypeStruct(hidden.shape, BF16),
            jax.ShapeDtypeStruct(gf.shape, BF16),
            jax.ShapeDtypeStruct((feat, width), F32),
            jax.ShapeDtypeStruct(gb.shape, F32),
        ),
        in_specs=[any_spec] * 4,
        out_specs=(any_spec,) * 4,
        scratch_shapes=[
            pltpu.VMEM(hidden.shape, BF16),
            pltpu.VMEM(gf.shape, BF16),
            pltpu.VMEM(gw.shape, BF16),
            pltpu.VMEM((feat, width), F32),
            pltpu.VMEM(gb.shape, F32),
            dma((4,)),
            dma((4,)),
        ],
        compiler_params=pltpu.CompilerParams(vmem_limit_bytes=60 * 1024 * 1024),
    )(*results)
    return hidden, gf, gw, gb.reshape(width)


def solution(mesh):
    in_specs = (
        P(("row", "col"), None),
        P(),
        P(),
        P("row", "col", None, None, None),
        P("row", "col", None),
        P("row", "col"),
        P(("col", "row"), None),
    )
    out_specs = (P(("col", "row"), None), P(("row", "col"), None), P(), P())
    body = functools.partial(local, mesh.shape["row"], mesh.shape["col"])
    return jax.shard_map(body, mesh=mesh, in_specs=in_specs, out_specs=out_specs, check_vma=False)
```

```python
import functools

import jax
import jax.numpy as jnp
from jax import lax
from jax.experimental import pallas as pl
from jax.experimental.pallas import tpu as pltpu
from jax.sharding import PartitionSpec as P

MESH = pl.DeviceIdType.MESH
F32 = jnp.float32
BF16 = jnp.bfloat16
GROUP = 16


def nearest_first(count):
    return sorted(range(1, count), key=lambda d: (min(d, count - d), d))


def remote(src, dst, send, recv, device):
    return pltpu.make_async_remote_copy(
        src_ref=src, dst_ref=dst, send_sem=send, recv_sem=recv, device_id=device, device_id_type=MESH
    )


def kernel(
    n_row, n_col, inner, split,
    features, weight, bias, tiles_in, index_in, count, cotangent,
    hidden_out, gf_out, gw_out, gb_out,
    x, w, b, tiles, adj, cot, hpart, hts, hid, dpre,
    ssend, srecv, zsend, zrecv, gsend, grecv, gfull, bparts, bouter, gb, gf, index,
    load_sem, store_sem, x_send, x_recv, c_send, c_recv, h_send, h_recv,
    s_send, s_recv, z_send, z_recv, g_send, g_recv, a_send, a_recv, b_send, b_recv, p_send, p_recv, d_send, d_recv,
):
    r = lax.axis_index("row")
    c = lax.axis_index("col")
    outer = n_col // inner
    hi = c // inner
    lo = lax.rem(c, inner)
    swap = lax.rem(r, 2) if outer == inner else 0
    a = hi + swap * (lo - hi)
    b_at = lo + swap * (hi - lo)

    def col_at(first, second):
        return (first + swap * (second - first)) * inner + second + swap * (first - second)

    def place_of(col):
        high, low = col // inner, lax.rem(col, inner)
        return (high + swap * (low - high)) * inner + low + swap * (high - low)

    me = a * inner + b_at
    rows = features.shape[0]
    own_rows = cot.shape[1]
    width = w.shape[1]
    slots, size = tiles.shape[0], tiles.shape[1]
    tile_cols = n_col * rows // size
    tile_rows = n_row * own_rows // size

    def block(spot):
        return pl.ds(pl.multiple_of(spot * rows, rows), rows)

    def turned(turn_a, turn_b):
        return lax.rem(a + turn_a, outer), lax.rem(b_at + turn_b, inner)

    def spot_of(turn_a, turn_b):
        first, second = turned(turn_a, turn_b)
        return first * inner + second

    def col_of(turn_a, turn_b):
        return col_at(*turned(turn_a, turn_b))

    load_x = pltpu.make_async_copy(features, x.at[block(me)], load_sem.at[0])
    load_c = pltpu.make_async_copy(cotangent, cot.at[r], load_sem.at[1])
    load_t = pltpu.make_async_copy(tiles_in.at[0, 0], tiles, load_sem.at[2])
    load_w = pltpu.make_async_copy(weight, w, load_sem.at[3])
    load_b = pltpu.make_async_copy(bias, b, load_sem.at[4])
    load_i = pltpu.make_async_copy(index_in, index, load_sem.at[5])
    for load in (load_x, load_c, load_t, load_w, load_b, load_i):
        load.start()

    barrier = pltpu.get_barrier_semaphore()
    for d in range(1, n_col):
        pl.semaphore_signal(barrier, inc=1, device_id=(r, lax.rem(c + d, n_col)), device_id_type=MESH)
    for d in range(1, n_row):
        pl.semaphore_signal(barrier, inc=1, device_id=(lax.rem(r + d, n_row), c), device_id_type=MESH)
    pl.semaphore_wait(barrier, n_col + n_row - 2)

    pending = []

    def send(copy):
        copy.start()
        pending.append(copy)

    def sent():
        for copy in pending:
            copy.wait_send()
        pending.clear()

    def send_x(number, source, to):
        send(remote(x.at[block(source)], x.at[block(source)], x_send.at[number], x_recv.at[source], (r, to)))

    def wait_x(source):
        remote(x.at[block(source)], x.at[block(source)], x_send.at[0], x_recv.at[source], (r, c)).wait_recv()

    number = 0
    load_x.wait()
    for d in nearest_first(outer):
        send_x(number, me, col_of(d, 0))
        number += 1
    for q in range(1, inner):
        send_x(number, me, col_of(0, q))
        number += 1
    load_c.wait()
    for d in range(1, n_row):
        send(remote(cot.at[r], cot.at[r], c_send.at[d], c_recv.at[r], (lax.rem(r + d, n_row), c)))

    load_t.wait()
    load_i.wait()
    live = count[0, 0]

    def place(t, carry):
        def find(s, slot):
            return jnp.where((index[0, 0, s] == t) & (s < live), s, slot)

        slot = lax.fori_loop(0, slots, find, jnp.int32(-1), unroll=min(slots, 16))
        tile = tiles[jnp.maximum(slot, 0)]
        row = pl.ds(pl.multiple_of(t // tile_cols * size, size), size)
        column = pl.ds(pl.multiple_of(place_of(lax.rem(t, tile_cols)) * size, size), size)
        adj[row, column] = jnp.where(slot >= 0, tile, jnp.zeros_like(tile))
        return carry

    places = tile_rows * tile_cols
    piece = places // outer
    for m, d in enumerate(nearest_first(outer)):
        lax.fori_loop(m * piece, (m + 1) * piece, place, 0)
        source = spot_of(d, 0)
        wait_x(source)
        for q in range(1, inner):
            send_x(number, source, col_of(0, q))
            number += 1
    lax.fori_loop((outer - 1) * piece, places, place, 0)
    span = inner * rows
    partial = None
    for d in [0] + nearest_first(outer):
        for q in range(1, inner):
            wait_x(spot_of(d, q))
        group = pl.ds(pl.multiple_of(lax.rem(a + d, outer) * span, span), span)
        part = jnp.dot(adj[:, group], x[group, :], preferred_element_type=F32)
        partial = part if partial is None else partial + part
    hpart[r] = partial
    for d in range(1, n_row):
        send(remote(hpart.at[r], hpart.at[r], h_send.at[d], h_recv.at[r], (lax.rem(r + d, n_row), c)))
    load_w.wait()
    load_b.wait()
    for d in range(1, n_row):
        other = lax.rem(r + d, n_row)
        remote(cot.at[other], cot.at[other], c_send.at[0], c_recv.at[other], (r, c)).wait_recv()
    for d in range(1, n_row):
        other = lax.rem(r + d, n_row)
        remote(hpart.at[other], hpart.at[other], h_send.at[0], h_recv.at[other], (r, c)).wait_recv()
    h = hpart[0]
    for k in range(1, n_row):
        h = h + hpart[k]
    hb = h.astype(BF16)
    hts[...] = h.T.astype(BF16)

    for k in range(n_row):
        part = hb[k * own_rows : (k + 1) * own_rows]
        pre = jnp.dot(part, w[...], preferred_element_type=F32) + b[...]
        sig = 0.5 * jnp.tanh(0.5 * pre) + 0.5
        hid[k] = (pre * sig).astype(BF16)
        grad = (cot[k].astype(F32) * (sig + pre * sig * (1.0 - sig))).astype(BF16)
        dpre[k * own_rows : (k + 1) * own_rows, :] = grad
    store_h = pltpu.make_async_copy(hid.at[r], hidden_out, store_sem.at[0])
    store_h.start()

    half = lax.rem(r, split)
    deep = hts.shape[0] // split
    gw = jnp.dot(hts[pl.ds(pl.multiple_of(half * deep, deep), deep), :], dpre[...], preferred_element_type=F32).astype(BF16)
    chunk = gsend.shape[2]
    parts = width // chunk
    for k in range(n_col):
        g, l = k // parts, k % parts
        gsend[k] = gw[g * GROUP : (g + 1) * GROUP, l * chunk : (l + 1) * chunk]
    grecv[c] = gsend[c]
    for d in range(1, n_col):
        to = lax.rem(c + d, n_col)
        send(remote(gsend.at[to], grecv.at[c], g_send.at[d], g_recv.at[c], (r, to)))

    gt = lax.dot_general(w[...], dpre[...], (((1,), (1,)), ((), ())), preferred_element_type=F32).astype(BF16)
    order = nearest_first(outer) + [0]
    portion = max(1, outer // 2)
    for n, d in enumerate(order):
        columns = pl.ds(pl.multiple_of(lax.rem(a + d, outer) * span, span), span)
        part = jnp.dot(gt, adj[:, columns], preferred_element_type=F32).astype(BF16)
        for q in range(inner):
            ssend[q, n] = part[:, q * rows : (q + 1) * rows]
        if (n + 1) % portion == 0:
            run, m = pl.ds(n + 1 - portion, portion), n // portion
            for q in range(1, inner):
                at = lax.rem(b_at + q, inner)
                send(remote(ssend.at[at, run], srecv.at[b_at, run], s_send.at[m, q], s_recv.at[m, b_at], (r, col_at(a, at))))
    bparts[lo] = jnp.sum(dpre[...].astype(F32), axis=0, keepdims=True)
    for q in range(1, inner):
        at = lax.rem(lo + q, inner)
        send(remote(bparts.at[lo], bparts.at[lo], b_send.at[q], b_recv.at[lo], (r, hi * inner + at)))

    for d in range(1, n_col):
        source = lax.rem(c + d, n_col)
        remote(gsend.at[0], grecv.at[source], g_send.at[0], g_recv.at[source], (r, c)).wait_recv()
    total = grecv[0].astype(F32)
    for k in range(1, n_col):
        total = total + grecv[k].astype(F32)
    gfull[half, c] = total.astype(BF16)
    for d in range(1, n_col):
        to = lax.rem(c + d, n_col)
        send(remote(gfull.at[half, c], gfull.at[half, c], a_send.at[d], a_recv.at[c], (r, to)))

    for q in range(1, inner):
        at = lax.rem(lo + q, inner)
        remote(bparts.at[at], bparts.at[at], b_send.at[0], b_recv.at[at], (r, c)).wait_recv()
    bias_sum = bparts[0]
    for q in range(1, inner):
        bias_sum = bias_sum + bparts[q]
    bouter[hi] = bias_sum
    for d in range(1, outer):
        to = lax.rem(hi + d, outer)
        send(remote(bouter.at[hi], bouter.at[hi], d_send.at[d], d_recv.at[hi], (r, to * inner + lo)))
    own_sum = None
    for n, d in enumerate(order):
        if n % portion == 0:
            run, m = pl.ds(n, portion), n // portion
            for q in range(1, inner):
                at = lax.rem(b_at + q, inner)
                remote(ssend.at[at, run], srecv.at[at, run], s_send.at[0, 0], s_recv.at[m, at], (r, c)).wait_recv()
        part = ssend[b_at, n].astype(F32)
        for q in range(1, inner):
            part = part + srecv[lax.rem(b_at + q, inner), n].astype(F32)
        if d:
            to = lax.rem(a + d, outer)
            zsend[d] = part.astype(BF16)
            send(remote(zsend.at[d], zrecv.at[a], z_send.at[d], z_recv.at[a], (r, col_at(to, b_at))))
        else:
            own_sum = part
    sent()
    for d in range(1, outer):
        source = lax.rem(hi + d, outer)
        remote(bouter.at[source], bouter.at[source], d_send.at[0], d_recv.at[source], (r, c)).wait_recv()
    bias_sum = bouter[0]
    for k in range(1, outer):
        bias_sum = bias_sum + bouter[k]
    gb[...] = bias_sum
    stores = [store_h]

    def store(source, target, sem):
        copy = pltpu.make_async_copy(source, target, store_sem.at[sem])
        copy.start()
        stores.append(copy)

    store(gb, gb_out, 1)
    for d in range(1, n_col):
        source = lax.rem(c + d, n_col)
        remote(gfull.at[half, source], gfull.at[half, source], a_send.at[0], a_recv.at[source], (r, c)).wait_recv()
    if split == 2:
        partner = r + 1 - 2 * half
        send(remote(gfull.at[half], gfull.at[half], p_send.at[0], p_recv.at[0], (partner, c)))
    store(gfull.at[half], gw_out.at[half], 2)
    for d in nearest_first(outer):
        source = lax.rem(a + d, outer)
        remote(zsend.at[0], zrecv.at[source], z_send.at[0], z_recv.at[source], (r, c)).wait_recv()
        own_sum = own_sum + zrecv[source].astype(F32)
    gf[...] = own_sum.T.astype(BF16)
    store(gf, gf_out, 3)
    if split == 2:
        remote(gfull.at[1 - half], gfull.at[1 - half], p_send.at[0], p_recv.at[0], (r, c)).wait_recv()
        store(gfull.at[1 - half], gw_out.at[1 - half], 4)
    sent()
    for copy in stores:
        copy.wait()


def hand_over(hidden_in, gf_in, gw_in, gb_in, hidden_out, gf_out, gw_out, gb_out, hidden, gf, gw, wide, gb, load_sem, store_sem):
    chunk = gw.shape[3]
    parts = wide.shape[1] // chunk
    deep = wide.shape[0] // gw.shape[0]
    moves = (
        (gw_in, gw, wide, gw_out),
        (hidden_in, hidden, hidden, hidden_out),
        (gf_in, gf, gf, gf_out),
        (gb_in, gb, gb, gb_out),
    )
    loads = [pltpu.make_async_copy(moves[k][0], moves[k][1], load_sem.at[k]) for k in range(4)]
    stores = [pltpu.make_async_copy(moves[k][2], moves[k][3], store_sem.at[k]) for k in range(4)]
    for load in loads:
        load.start()
    for k in range(4):
        loads[k].wait()
        if k == 0:
            for n in range(gw.shape[0]):
                for m in range(gw.shape[1]):
                    top, l = n * deep + m // parts * GROUP, m % parts
                    wide[top : top + GROUP, l * chunk : (l + 1) * chunk] = gw[n, m].astype(F32)
        stores[k].start()
    for copy in stores:
        copy.wait()


def local(n_row, n_col, features, weight, bias, tile_values, tile_index, tile_count, cotangent):
    rows, feat = features.shape
    own_rows, width = cotangent.shape
    slots, size = tile_values.shape[2], tile_values.shape[3]
    inner = 4
    outer = n_col // inner
    target = n_row * own_rows
    source = n_col * rows
    chunk = feat * width // (GROUP * n_col)
    split = 1
    chunk = chunk // split
    dma = pltpu.SemaphoreType.DMA
    any_spec = pl.BlockSpec(memory_space=pl.ANY)
    hbm = pl.BlockSpec(memory_space=pltpu.HBM)
    hidden, gf, gw, gb = pl.pallas_call(
        functools.partial(kernel, n_row, n_col, inner, split),
        out_shape=(
            jax.ShapeDtypeStruct((own_rows, width), BF16),
            jax.ShapeDtypeStruct((rows, feat), BF16),
            jax.ShapeDtypeStruct((split, n_col, GROUP, chunk), BF16),
            jax.ShapeDtypeStruct((1, width), F32),
        ),
        in_specs=[hbm] * 5 + [pl.BlockSpec(memory_space=pltpu.SMEM), hbm],
        out_specs=(any_spec,) * 4,
        scratch_shapes=[
            pltpu.VMEM((source, feat), BF16),
            pltpu.VMEM((feat, width), BF16),
            pltpu.VMEM((1, width), F32),
            pltpu.VMEM((slots, size, size), BF16),
            pltpu.VMEM((target, source), BF16),
            pltpu.VMEM((n_row, own_rows, width), BF16),
            pltpu.VMEM((n_row, target, feat), F32),
            pltpu.VMEM((feat, target), BF16),
            pltpu.VMEM((n_row, own_rows, width), BF16),
            pltpu.VMEM((target, width), BF16),
            pltpu.VMEM((inner, outer, feat, rows), BF16),
            pltpu.VMEM((inner, outer, feat, rows), BF16),
            pltpu.VMEM((outer, feat, rows), BF16),
            pltpu.VMEM((outer, feat, rows), BF16),
            pltpu.VMEM((n_col, GROUP, chunk), BF16),
            pltpu.VMEM((n_col, GROUP, chunk), BF16),
            pltpu.VMEM((split, n_col, GROUP, chunk), BF16),
            pltpu.VMEM((inner, 1, width), F32),
            pltpu.VMEM((outer, 1, width), F32),
            pltpu.VMEM((1, width), F32),
            pltpu.VMEM((rows, feat), BF16),
            pltpu.SMEM(tile_index.shape, jnp.int32),
            dma((6,)), dma((5,)),
            dma((n_col,)), dma((n_col,)),
            dma((n_row,)), dma((n_row,)),
            dma((n_row,)), dma((n_row,)),
            dma((outer, inner)), dma((outer, inner)),
            dma((outer,)), dma((outer,)),
            dma((n_col,)), dma((n_col,)),
            dma((n_col,)), dma((n_col,)),
            dma((n_col,)), dma((n_col,)),
            dma((1,)), dma((1,)),
            dma((outer,)), dma((outer,)),
        ],
        compiler_params=pltpu.CompilerParams(
            collective_id=0, has_side_effects=True, vmem_limit_bytes=60 * 1024 * 1024
        ),
        cost_estimate=pl.CostEstimate(
            flops=4 * target * source * feat + 6 * target * width * feat,
            bytes_accessed=2 * (slots * size * size + 3 * own_rows * width),
            transcendentals=target * width,
        ),
    )(features, weight, bias.reshape(1, width), tile_values, tile_index, tile_count, cotangent)
    results = (hidden, gf, gw, gb)
    hidden, gf, gw, gb = pl.pallas_call(
        hand_over,
        out_shape=(
            jax.ShapeDtypeStruct(hidden.shape, BF16),
            jax.ShapeDtypeStruct(gf.shape, BF16),
            jax.ShapeDtypeStruct((feat, width), F32),
            jax.ShapeDtypeStruct(gb.shape, F32),
        ),
        in_specs=[any_spec] * 4,
        out_specs=(any_spec,) * 4,
        scratch_shapes=[
            pltpu.VMEM(hidden.shape, BF16),
            pltpu.VMEM(gf.shape, BF16),
            pltpu.VMEM(gw.shape, BF16),
            pltpu.VMEM((feat, width), F32),
            pltpu.VMEM(gb.shape, F32),
            dma((4,)),
            dma((4,)),
        ],
        compiler_params=pltpu.CompilerParams(vmem_limit_bytes=60 * 1024 * 1024),
    )(*results)
    return hidden, gf, gw, gb.reshape(width)


def solution(mesh):
    in_specs = (
        P(("row", "col"), None),
        P(),
        P(),
        P("row", "col", None, None, None),
        P("row", "col", None),
        P("row", "col"),
        P(("col", "row"), None),
    )
    out_specs = (P(("col", "row"), None), P(("row", "col"), None), P(), P())
    body = functools.partial(local, mesh.shape["row"], mesh.shape["col"])
    return jax.shard_map(body, mesh=mesh, in_specs=in_specs, out_specs=out_specs, check_vma=False)
```

```python
import functools

import jax
import jax.numpy as jnp
from jax import lax
from jax.experimental import pallas as pl
from jax.experimental.pallas import tpu as pltpu
from jax.sharding import PartitionSpec as P

MESH = pl.DeviceIdType.MESH
F32 = jnp.float32
BF16 = jnp.bfloat16
GROUP = 16


def nearest_first(count):
    return sorted(range(1, count), key=lambda d: (min(d, count - d), d))


def remote(src, dst, send, recv, device):
    return pltpu.make_async_remote_copy(
        src_ref=src, dst_ref=dst, send_sem=send, recv_sem=recv, device_id=device, device_id_type=MESH
    )


def kernel(
    n_row, n_col, inner, split,
    features, weight, bias, tiles_in, index_in, count, cotangent,
    hidden_out, gf_out, gw_out, gb_out,
    x, w, b, tiles, adj, cot, hpart, hts, hid, dpre,
    ssend, srecv, zsend, zrecv, gsend, grecv, gfull, bparts, bouter, gb, gf, index,
    load_sem, store_sem, x_send, x_recv, c_send, c_recv, h_send, h_recv,
    s_send, s_recv, z_send, z_recv, g_send, g_recv, a_send, a_recv, b_send, b_recv, p_send, p_recv, d_send, d_recv,
):
    r = lax.axis_index("row")
    c = lax.axis_index("col")
    outer = n_col // inner
    hi = c // inner
    lo = lax.rem(c, inner)
    swap = lax.rem(r, 2) if outer == inner else 0
    a = hi + swap * (lo - hi)
    b_at = lo + swap * (hi - lo)

    def col_at(first, second):
        return (first + swap * (second - first)) * inner + second + swap * (first - second)

    def place_of(col):
        high, low = col // inner, lax.rem(col, inner)
        return (high + swap * (low - high)) * inner + low + swap * (high - low)

    me = a * inner + b_at
    rows = features.shape[0]
    own_rows = cot.shape[1]
    width = w.shape[1]
    slots, size = tiles.shape[0], tiles.shape[1]
    tile_cols = n_col * rows // size
    tile_rows = n_row * own_rows // size

    def block(spot):
        return pl.ds(pl.multiple_of(spot * rows, rows), rows)

    def turned(turn_a, turn_b):
        return lax.rem(a + turn_a, outer), lax.rem(b_at + turn_b, inner)

    def spot_of(turn_a, turn_b):
        first, second = turned(turn_a, turn_b)
        return first * inner + second

    def col_of(turn_a, turn_b):
        return col_at(*turned(turn_a, turn_b))

    load_x = pltpu.make_async_copy(features, x.at[block(me)], load_sem.at[0])
    load_c = pltpu.make_async_copy(cotangent, cot.at[r], load_sem.at[1])
    load_t = pltpu.make_async_copy(tiles_in.at[0, 0], tiles, load_sem.at[2])
    load_w = pltpu.make_async_copy(weight, w, load_sem.at[3])
    load_b = pltpu.make_async_copy(bias, b, load_sem.at[4])
    load_i = pltpu.make_async_copy(index_in, index, load_sem.at[5])
    for load in (load_x, load_c, load_t, load_w, load_b, load_i):
        load.start()

    barrier = pltpu.get_barrier_semaphore()
    for d in range(1, n_col):
        pl.semaphore_signal(barrier, inc=1, device_id=(r, lax.rem(c + d, n_col)), device_id_type=MESH)
    for d in range(1, n_row):
        pl.semaphore_signal(barrier, inc=1, device_id=(lax.rem(r + d, n_row), c), device_id_type=MESH)
    pl.semaphore_wait(barrier, n_col + n_row - 2)

    pending = []

    def send(copy):
        copy.start()
        pending.append(copy)

    def sent():
        for copy in pending:
            copy.wait_send()
        pending.clear()

    def send_x(number, source, to):
        send(remote(x.at[block(source)], x.at[block(source)], x_send.at[number], x_recv.at[source], (r, to)))

    def wait_x(source):
        remote(x.at[block(source)], x.at[block(source)], x_send.at[0], x_recv.at[source], (r, c)).wait_recv()

    number = 0
    load_x.wait()
    for d in nearest_first(outer):
        send_x(number, me, col_of(d, 0))
        number += 1
    for q in range(1, inner):
        send_x(number, me, col_of(0, q))
        number += 1
    load_c.wait()
    for d in range(1, n_row):
        send(remote(cot.at[r], cot.at[r], c_send.at[d], c_recv.at[r], (lax.rem(r + d, n_row), c)))

    load_t.wait()
    load_i.wait()
    live = count[0, 0]

    def place(t, carry):
        def find(s, slot):
            return jnp.where((index[0, 0, s] == t) & (s < live), s, slot)

        slot = lax.fori_loop(0, slots, find, jnp.int32(-1), unroll=min(slots, 16))
        tile = tiles[jnp.maximum(slot, 0)]
        row = pl.ds(pl.multiple_of(t // tile_cols * size, size), size)
        column = pl.ds(pl.multiple_of(place_of(lax.rem(t, tile_cols)) * size, size), size)
        adj[row, column] = jnp.where(slot >= 0, tile, jnp.zeros_like(tile))
        return carry

    places = tile_rows * tile_cols
    piece = places // outer
    for m, d in enumerate(nearest_first(outer)):
        lax.fori_loop(m * piece, (m + 1) * piece, place, 0)
        source = spot_of(d, 0)
        wait_x(source)
        for q in range(1, inner):
            send_x(number, source, col_of(0, q))
            number += 1
    lax.fori_loop((outer - 1) * piece, places, place, 0)
    span = inner * rows
    partial = None
    for d in [0] + nearest_first(outer):
        for q in range(1, inner):
            wait_x(spot_of(d, q))
        group = pl.ds(pl.multiple_of(lax.rem(a + d, outer) * span, span), span)
        part = jnp.dot(adj[:, group], x[group, :], preferred_element_type=F32)
        partial = part if partial is None else partial + part
    hpart[r] = partial
    for d in range(1, n_row):
        send(remote(hpart.at[r], hpart.at[r], h_send.at[d], h_recv.at[r], (lax.rem(r + d, n_row), c)))
    load_w.wait()
    load_b.wait()
    for d in range(1, n_row):
        other = lax.rem(r + d, n_row)
        remote(cot.at[other], cot.at[other], c_send.at[0], c_recv.at[other], (r, c)).wait_recv()
    for d in range(1, n_row):
        other = lax.rem(r + d, n_row)
        remote(hpart.at[other], hpart.at[other], h_send.at[0], h_recv.at[other], (r, c)).wait_recv()
    h = hpart[0]
    for k in range(1, n_row):
        h = h + hpart[k]
    hb = h.astype(BF16)
    hts[...] = h.T.astype(BF16)

    for k in range(n_row):
        part = hb[k * own_rows : (k + 1) * own_rows]
        pre = jnp.dot(part, w[...], preferred_element_type=F32) + b[...]
        sig = 0.5 * jnp.tanh(0.5 * pre) + 0.5
        hid[k] = (pre * sig).astype(BF16)
        grad = (cot[k].astype(F32) * (sig + pre * sig * (1.0 - sig))).astype(BF16)
        dpre[k * own_rows : (k + 1) * own_rows, :] = grad
    store_h = pltpu.make_async_copy(hid.at[r], hidden_out, store_sem.at[0])
    store_h.start()

    gt = lax.dot_general(w[...], dpre[...], (((1,), (1,)), ((), ())), preferred_element_type=F32).astype(BF16)
    order = nearest_first(outer) + [0]
    portion = max(1, outer // 2)
    for n, d in enumerate(order):
        columns = pl.ds(pl.multiple_of(lax.rem(a + d, outer) * span, span), span)
        part = jnp.dot(gt, adj[:, columns], preferred_element_type=F32).astype(BF16)
        for q in range(inner):
            ssend[q, n] = part[:, q * rows : (q + 1) * rows]
        if (n + 1) % portion == 0:
            run, m = pl.ds(n + 1 - portion, portion), n // portion
            for q in range(1, inner):
                at = lax.rem(b_at + q, inner)
                send(remote(ssend.at[at, run], srecv.at[b_at, run], s_send.at[m, q], s_recv.at[m, b_at], (r, col_at(a, at))))
    half = lax.rem(r, split)
    deep = hts.shape[0] // split
    gw = jnp.dot(hts[pl.ds(pl.multiple_of(half * deep, deep), deep), :], dpre[...], preferred_element_type=F32).astype(BF16)
    chunk = gsend.shape[2]
    parts = width // chunk
    for k in range(n_col):
        g, l = k // parts, k % parts
        gsend[k] = gw[g * GROUP : (g + 1) * GROUP, l * chunk : (l + 1) * chunk]
    grecv[c] = gsend[c]
    for d in range(1, n_col):
        to = lax.rem(c + d, n_col)
        send(remote(gsend.at[to], grecv.at[c], g_send.at[d], g_recv.at[c], (r, to)))

    bparts[lo] = jnp.sum(dpre[...].astype(F32), axis=0, keepdims=True)
    for q in range(1, inner):
        at = lax.rem(lo + q, inner)
        send(remote(bparts.at[lo], bparts.at[lo], b_send.at[q], b_recv.at[lo], (r, hi * inner + at)))

    for d in range(1, n_col):
        source = lax.rem(c + d, n_col)
        remote(gsend.at[0], grecv.at[source], g_send.at[0], g_recv.at[source], (r, c)).wait_recv()
    total = grecv[0].astype(F32)
    for k in range(1, n_col):
        total = total + grecv[k].astype(F32)
    gfull[half, c] = total.astype(BF16)
    for d in range(1, n_col):
        to = lax.rem(c + d, n_col)
        send(remote(gfull.at[half, c], gfull.at[half, c], a_send.at[d], a_recv.at[c], (r, to)))

    for q in range(1, inner):
        at = lax.rem(lo + q, inner)
        remote(bparts.at[at], bparts.at[at], b_send.at[0], b_recv.at[at], (r, c)).wait_recv()
    bias_sum = bparts[0]
    for q in range(1, inner):
        bias_sum = bias_sum + bparts[q]
    bouter[hi] = bias_sum
    for d in range(1, outer):
        to = lax.rem(hi + d, outer)
        send(remote(bouter.at[hi], bouter.at[hi], d_send.at[d], d_recv.at[hi], (r, to * inner + lo)))
    own_sum = None
    for n, d in enumerate(order):
        if n % portion == 0:
            run, m = pl.ds(n, portion), n // portion
            for q in range(1, inner):
                at = lax.rem(b_at + q, inner)
                remote(ssend.at[at, run], srecv.at[at, run], s_send.at[0, 0], s_recv.at[m, at], (r, c)).wait_recv()
        part = ssend[b_at, n].astype(F32)
        for q in range(1, inner):
            part = part + srecv[lax.rem(b_at + q, inner), n].astype(F32)
        if d:
            to = lax.rem(a + d, outer)
            zsend[d] = part.astype(BF16)
            send(remote(zsend.at[d], zrecv.at[a], z_send.at[d], z_recv.at[a], (r, col_at(to, b_at))))
        else:
            own_sum = part
    sent()
    for d in range(1, outer):
        source = lax.rem(hi + d, outer)
        remote(bouter.at[source], bouter.at[source], d_send.at[0], d_recv.at[source], (r, c)).wait_recv()
    bias_sum = bouter[0]
    for k in range(1, outer):
        bias_sum = bias_sum + bouter[k]
    gb[...] = bias_sum
    stores = [store_h]

    def store(source, target, sem):
        copy = pltpu.make_async_copy(source, target, store_sem.at[sem])
        copy.start()
        stores.append(copy)

    store(gb, gb_out, 1)
    for d in range(1, n_col):
        source = lax.rem(c + d, n_col)
        remote(gfull.at[half, source], gfull.at[half, source], a_send.at[0], a_recv.at[source], (r, c)).wait_recv()
    if split == 2:
        partner = r + 1 - 2 * half
        send(remote(gfull.at[half], gfull.at[half], p_send.at[0], p_recv.at[0], (partner, c)))
    store(gfull.at[half], gw_out.at[half], 2)
    for d in nearest_first(outer):
        source = lax.rem(a + d, outer)
        remote(zsend.at[0], zrecv.at[source], z_send.at[0], z_recv.at[source], (r, c)).wait_recv()
        own_sum = own_sum + zrecv[source].astype(F32)
    gf[...] = own_sum.T.astype(BF16)
    store(gf, gf_out, 3)
    if split == 2:
        remote(gfull.at[1 - half], gfull.at[1 - half], p_send.at[0], p_recv.at[0], (r, c)).wait_recv()
        store(gfull.at[1 - half], gw_out.at[1 - half], 4)
    sent()
    for copy in stores:
        copy.wait()


def hand_over(hidden_in, gf_in, gw_in, gb_in, hidden_out, gf_out, gw_out, gb_out, hidden, gf, gw, wide, gb, load_sem, store_sem):
    chunk = gw.shape[3]
    parts = wide.shape[1] // chunk
    deep = wide.shape[0] // gw.shape[0]
    moves = (
        (gw_in, gw, wide, gw_out),
        (hidden_in, hidden, hidden, hidden_out),
        (gf_in, gf, gf, gf_out),
        (gb_in, gb, gb, gb_out),
    )
    loads = [pltpu.make_async_copy(moves[k][0], moves[k][1], load_sem.at[k]) for k in range(4)]
    stores = [pltpu.make_async_copy(moves[k][2], moves[k][3], store_sem.at[k]) for k in range(4)]
    for load in loads:
        load.start()
    for k in range(4):
        loads[k].wait()
        if k == 0:
            for n in range(gw.shape[0]):
                for m in range(gw.shape[1]):
                    top, l = n * deep + m // parts * GROUP, m % parts
                    wide[top : top + GROUP, l * chunk : (l + 1) * chunk] = gw[n, m].astype(F32)
        stores[k].start()
    for copy in stores:
        copy.wait()


def local(n_row, n_col, features, weight, bias, tile_values, tile_index, tile_count, cotangent):
    rows, feat = features.shape
    own_rows, width = cotangent.shape
    slots, size = tile_values.shape[2], tile_values.shape[3]
    inner = 4
    outer = n_col // inner
    target = n_row * own_rows
    source = n_col * rows
    chunk = feat * width // (GROUP * n_col)
    split = 2 if n_row % 2 == 0 and chunk % 256 == 0 else 1
    chunk = chunk // split
    dma = pltpu.SemaphoreType.DMA
    any_spec = pl.BlockSpec(memory_space=pl.ANY)
    hbm = pl.BlockSpec(memory_space=pltpu.HBM)
    hidden, gf, gw, gb = pl.pallas_call(
        functools.partial(kernel, n_row, n_col, inner, split),
        out_shape=(
            jax.ShapeDtypeStruct((own_rows, width), BF16),
            jax.ShapeDtypeStruct((rows, feat), BF16),
            jax.ShapeDtypeStruct((split, n_col, GROUP, chunk), BF16),
            jax.ShapeDtypeStruct((1, width), F32),
        ),
        in_specs=[hbm] * 5 + [pl.BlockSpec(memory_space=pltpu.SMEM), hbm],
        out_specs=(any_spec,) * 4,
        scratch_shapes=[
            pltpu.VMEM((source, feat), BF16),
            pltpu.VMEM((feat, width), BF16),
            pltpu.VMEM((1, width), F32),
            pltpu.VMEM((slots, size, size), BF16),
            pltpu.VMEM((target, source), BF16),
            pltpu.VMEM((n_row, own_rows, width), BF16),
            pltpu.VMEM((n_row, target, feat), F32),
            pltpu.VMEM((feat, target), BF16),
            pltpu.VMEM((n_row, own_rows, width), BF16),
            pltpu.VMEM((target, width), BF16),
            pltpu.VMEM((inner, outer, feat, rows), BF16),
            pltpu.VMEM((inner, outer, feat, rows), BF16),
            pltpu.VMEM((outer, feat, rows), BF16),
            pltpu.VMEM((outer, feat, rows), BF16),
            pltpu.VMEM((n_col, GROUP, chunk), BF16),
            pltpu.VMEM((n_col, GROUP, chunk), BF16),
            pltpu.VMEM((split, n_col, GROUP, chunk), BF16),
            pltpu.VMEM((inner, 1, width), F32),
            pltpu.VMEM((outer, 1, width), F32),
            pltpu.VMEM((1, width), F32),
            pltpu.VMEM((rows, feat), BF16),
            pltpu.SMEM(tile_index.shape, jnp.int32),
            dma((6,)), dma((5,)),
            dma((n_col,)), dma((n_col,)),
            dma((n_row,)), dma((n_row,)),
            dma((n_row,)), dma((n_row,)),
            dma((outer, inner)), dma((outer, inner)),
            dma((outer,)), dma((outer,)),
            dma((n_col,)), dma((n_col,)),
            dma((n_col,)), dma((n_col,)),
            dma((n_col,)), dma((n_col,)),
            dma((1,)), dma((1,)),
            dma((outer,)), dma((outer,)),
        ],
        compiler_params=pltpu.CompilerParams(
            collective_id=0, has_side_effects=True, vmem_limit_bytes=60 * 1024 * 1024
        ),
        cost_estimate=pl.CostEstimate(
            flops=4 * target * source * feat + 6 * target * width * feat,
            bytes_accessed=2 * (slots * size * size + 3 * own_rows * width),
            transcendentals=target * width,
        ),
    )(features, weight, bias.reshape(1, width), tile_values, tile_index, tile_count, cotangent)
    results = (hidden, gf, gw, gb)
    hidden, gf, gw, gb = pl.pallas_call(
        hand_over,
        out_shape=(
            jax.ShapeDtypeStruct(hidden.shape, BF16),
            jax.ShapeDtypeStruct(gf.shape, BF16),
            jax.ShapeDtypeStruct((feat, width), F32),
            jax.ShapeDtypeStruct(gb.shape, F32),
        ),
        in_specs=[any_spec] * 4,
        out_specs=(any_spec,) * 4,
        scratch_shapes=[
            pltpu.VMEM(hidden.shape, BF16),
            pltpu.VMEM(gf.shape, BF16),
            pltpu.VMEM(gw.shape, BF16),
            pltpu.VMEM((feat, width), F32),
            pltpu.VMEM(gb.shape, F32),
            dma((4,)),
            dma((4,)),
        ],
        compiler_params=pltpu.CompilerParams(vmem_limit_bytes=60 * 1024 * 1024),
    )(*results)
    return hidden, gf, gw, gb.reshape(width)


def solution(mesh):
    in_specs = (
        P(("row", "col"), None),
        P(),
        P(),
        P("row", "col", None, None, None),
        P("row", "col", None),
        P("row", "col"),
        P(("col", "row"), None),
    )
    out_specs = (P(("col", "row"), None), P(("row", "col"), None), P(), P())
    body = functools.partial(local, mesh.shape["row"], mesh.shape["col"])
    return jax.shard_map(body, mesh=mesh, in_specs=in_specs, out_specs=out_specs, check_vma=False)
```
